256 devices in a mesh: dp: 8 (over z), fsdp: 32 (over x, y, core).
Axes of the slice: x: 4, y: 4, z: 8, core: 2. Of those that a mesh axis runs over, the one named last changes fastest.
Arguments:
- queries: bfloat16 [2048, 32, 128], P(('dp', 'fsdp')), may hold values from -0.625 to 0.625
- passages: bfloat16 [512, 512, 128], P(('dp', 'fsdp')), may hold values from -0.625 to 0.625
- lengths: int32 [512], P(('dp', 'fsdp')), may hold values from 128 to 512, as said below
- pos_ids: int32 [2048], P(('dp', 'fsdp')), may hold values from 0 to 63
- neg_ids: int32 [2048, 4], P(('dp', 'fsdp')), may hold values from 0 to 511, as said below
Outputs:
- loss_rows: float32 [2048], P(('dp', 'fsdp'))
- query_grad: bfloat16 [2048, 32, 128], P(('dp', 'fsdp'))
- passage_grad: bfloat16 [512, 512, 128], P(('dp', 'fsdp'))
The draws below stay inside these ranges and needn't reach their ends.
Inputs may be any that keep to these rules, and one draw needn't show every extreme that they name: `lengths`: the first passage of each aligned run of 4 devices has all 512 slots valid. `neg_ids`: the 4 negatives of a query are distinct passages of other groups, each on the device with the same fsdp index as the query's device.
All inputs are finite; a program needn't handle non-finite values.
Results may differ from the reference program's by a relative error of at most 0.008.
Values may be sent and summed in bfloat16 or wider, within the bound.
No kernel may reach another device: no remote copies, remote signals or barrier semaphores. Data moves between devices by JAX's collectives and lax.ppermute only.
A program may use at most 128 MiB of HBM per device.

```python
import jax
import jax.numpy as jnp
from jax import lax

D = 128
QT = 32
LMAX = 512
MINLEN = 128
NEG = 4
QD = 8
PD = 2
QUERIES = 2048
PASSAGES = 512
N_DP = 8
N_FSDP = 32


def draw_queries(key, part):
    key = jax.random.fold_in(key, 7)
    return jnp.clip(0.09 * jax.random.normal(key, (QUERIES, QT, D), jnp.float32), -0.625, 0.625).astype(jnp.bfloat16)


def draw_passages(key, part):
    key = jax.random.fold_in(key, 9)
    return jnp.clip(0.09 * jax.random.normal(key, (PASSAGES, LMAX, D), jnp.float32), -0.625, 0.625).astype(jnp.bfloat16)


def draw_lengths(key, part):
    key = jax.random.fold_in(key, 3)
    drawn = jax.random.randint(key, (PASSAGES,), MINLEN, LMAX + 1)
    slots = jnp.arange(PASSAGES, dtype=jnp.int32)
    return jnp.where(slots % (4 * PD) == 0, LMAX, drawn).astype(jnp.int32)


def draw_neg_ids(key, part):
    key = jax.random.fold_in(key, 5)
    rows = jnp.arange(QUERIES, dtype=jnp.int32)
    group = rows // (QD * N_FSDP)
    member = rows // QD % N_FSDP
    candidates = (N_DP - 1) * PD
    ranks = jax.random.randint(key, (QUERIES, candidates), 0, 65536) * candidates
    ranks = ranks + jnp.arange(candidates, dtype=jnp.int32)[None, :]
    picked = jnp.argsort(ranks, axis=1)[:, :NEG].astype(jnp.int32)
    offset = 1 + picked // PD
    slot = picked % PD
    other = (group[:, None] + offset) % N_DP
    return (other * (PD * N_FSDP) + member[:, None] * PD + slot).astype(jnp.int32)


def with_ends(array, stream_key, smallest, high):
    shape = array.shape
    index_at = [jax.random.randint(jax.random.fold_in(stream_key, axis), (), 0, shape[axis]) for axis in range(len(shape))]
    array = array.at[tuple(index_at)].set(smallest)
    longest = shape.index(max(shape))
    index_at[longest] = (index_at[longest] + 1) % shape[longest]
    return array.at[tuple(index_at)].set(high)


def setup_inputs(seed: int = 0) -> dict:
    streams_of = jax.random.split(jax.random.key(seed), 6)
    queries = draw_queries(jax.random.fold_in(streams_of[5], 71), 0)
    passages = draw_passages(jax.random.fold_in(streams_of[5], 71), 0)
    lengths = draw_lengths(jax.random.fold_in(streams_of[5], 71), 0)
    pos_ids = with_ends(jax.random.randint(streams_of[3], (QUERIES,), 0, N_FSDP * PD), jax.random.fold_in(streams_of[3], 1), 0, (N_FSDP * PD) - 1).astype(jnp.int32)
    neg_ids = draw_neg_ids(jax.random.fold_in(streams_of[5], 71), 0)
    return {"queries": queries, "passages": passages, "lengths": lengths, "pos_ids": pos_ids, "neg_ids": neg_ids}


sharpness_divisor = 0.1


def token_stats(q, p, usable_entry_flags):
    affinity_matrix = jnp.einsum("atd,bud->abtu", q.astype(jnp.float32), p.astype(jnp.float32))
    sharpened_affinities = jnp.where(usable_entry_flags[None, :, None, :], affinity_matrix / sharpness_divisor, -1e30)
    largest_affinity = jnp.max(sharpened_affinities, axis=3, keepdims=True)
    exponential_entries = jnp.exp(sharpened_affinities - largest_affinity)
    normalizer_total = jnp.sum(exponential_entries, axis=3, keepdims=True)
    return sharpness_divisor * (largest_affinity[..., 0] + jnp.log(normalizer_total[..., 0])), exponential_entries / normalizer_total


def pair_stats(q, p, usable_entry_flags):
    affinity_matrix = jnp.einsum("atd,anud->antu", q.astype(jnp.float32), p.astype(jnp.float32))
    sharpened_affinities = jnp.where(usable_entry_flags[:, :, None, :], affinity_matrix / sharpness_divisor, -1e30)
    largest_affinity = jnp.max(sharpened_affinities, axis=3, keepdims=True)
    exponential_entries = jnp.exp(sharpened_affinities - largest_affinity)
    normalizer_total = jnp.sum(exponential_entries, axis=3, keepdims=True)
    return sharpness_divisor * (largest_affinity[..., 0] + jnp.log(normalizer_total[..., 0])), exponential_entries / normalizer_total


def softmax_terms(in_scores, neg_scores, pos):
    hot = jnp.arange(in_scores.shape[1], dtype=jnp.int32)[None, :] == pos[:, None]
    largest_affinity = jnp.maximum(jnp.max(in_scores, axis=1, keepdims=True), jnp.max(neg_scores, axis=1, keepdims=True))
    ein = jnp.exp(in_scores - largest_affinity)
    eneg = jnp.exp(neg_scores - largest_affinity)
    normalizer_total = jnp.sum(ein, axis=1, keepdims=True) + jnp.sum(eneg, axis=1, keepdims=True)
    loss = largest_affinity[:, 0] + jnp.log(normalizer_total[:, 0]) - jnp.sum(jnp.where(hot, in_scores, 0.0), axis=1)
    return loss, ein / normalizer_total - hot.astype(jnp.float32), eneg / normalizer_total


def reference(queries, passages, lengths, pos_ids, neg_ids):
    group_q = QD * N_FSDP
    group_p = PD * N_FSDP
    usable_entry_flags = jnp.arange(LMAX, dtype=jnp.int32)[None, :] < lengths[:, None]

    def step(carry, index):
        group = (index // N_FSDP).astype(jnp.int32)
        start = (group * group_p).astype(jnp.int32)
        qrows = lax.dynamic_slice_in_dim(queries, (index * QD).astype(jnp.int32), QD, 0)
        prows = lax.dynamic_slice_in_dim(passages, start, group_p, 0)
        pvalid = lax.dynamic_slice_in_dim(usable_entry_flags, start, group_p, 0)
        ids = lax.dynamic_slice_in_dim(neg_ids, (index * QD).astype(jnp.int32), QD, 0)
        pos = lax.dynamic_slice_in_dim(pos_ids, (index * QD).astype(jnp.int32), QD, 0)
        neg_p = passages[ids]
        neg_valid = usable_entry_flags[ids]
        maxsim, weight = token_stats(qrows, prows, pvalid)
        neg_maxsim, neg_weight = pair_stats(qrows, neg_p, neg_valid)
        loss, dl_in, dl_neg = softmax_terms(jnp.sum(maxsim, axis=2), jnp.sum(neg_maxsim, axis=2), pos)
        grad_in = (dl_in[:, :, None, None] * weight).astype(jnp.bfloat16).astype(jnp.float32)
        grad_neg = (dl_neg[:, :, None, None] * neg_weight).astype(jnp.bfloat16).astype(jnp.float32)
        dq = jnp.einsum("abtu,bud->atd", grad_in, prows.astype(jnp.float32))
        dq = dq + jnp.einsum("antu,anud->atd", grad_neg, neg_p.astype(jnp.float32))
        dp_in = jnp.einsum("abtu,atd->bud", grad_in, qrows.astype(jnp.float32))
        dp_neg = jnp.einsum("antu,atd->anud", grad_neg, qrows.astype(jnp.float32))
        old = lax.dynamic_slice_in_dim(carry, start, group_p, 0)
        carry = lax.dynamic_update_slice_in_dim(carry, old + dp_in, start, 0)
        carry = carry.at[ids.reshape(-1)].add(dp_neg.reshape(-1, LMAX, D))
        return carry, (loss, dq.astype(jnp.bfloat16))

    init = jnp.zeros((PASSAGES, LMAX, D), jnp.float32)
    dp_total, (losses, dqs) = lax.scan(step, init, jnp.arange(QUERIES // QD, dtype=jnp.int32))
    return losses.reshape(QUERIES), dqs.reshape(QUERIES, QT, D), dp_total.astype(jnp.bfloat16)
```

```python
import functools
import math

import jax
import jax.numpy as jnp
from jax import lax
from jax.experimental import pallas as pl
from jax.experimental.pallas import tpu as pltpu
from jax.sharding import PartitionSpec as P

F32, BF16 = jnp.float32, jnp.bfloat16
X, Y, C, Z = 4, 4, 2, 8
QN, QT, W, SLOTS, META = 8, 32, 128, 512, 16
QR = QN * QT
CH = 8
TEMP = 0.1
SCALE = 1.0 / TEMP * math.log2(math.e)
LOW = -1e30
ZORDER = (0, 4, 2, 6, 1, 5, 3, 7)
PARAMS = pltpu.CompilerParams(vmem_limit_bytes=48 * 1024 * 1024)
NT = (((1,), (1,)), ((), ()))


def index(x, y, c):
    return ((x % X) * Y + (y % Y)) * C + c


def along(value, dx=0, dy=0, swap=0):
    pairs = [
        (index(x, y, c), index(x + dx, y + dy, c ^ swap))
        for x in range(X) for y in range(Y) for c in range(C)
    ]
    return lax.ppermute(value, "fsdp", pairs)


def along_z(value, flip):
    return lax.ppermute(value, "dp", [(z, z ^ flip) for z in range(Z)])


def whole(shape, start=None):
    start = (0,) * len(shape) if start is None else start
    return pl.BlockSpec(shape, lambda *_: start)


def call(body, outs, in_specs, out_specs=None, grid=None, name=None, flops=0, moved=0, exps=0):
    grid = (1,) if grid is None else grid
    return pl.pallas_call(
        body,
        out_shape=[jax.ShapeDtypeStruct(s, d) for s, d in outs],
        in_specs=in_specs,
        out_specs=[whole(s) for s, _ in outs] if out_specs is None else out_specs,
        compiler_params=PARAMS,
        cost_estimate=pl.CostEstimate(flops=flops, bytes_accessed=moved, transcendentals=exps),
        name=name,
        grid=grid,
    )


def pack_body(q_ref, p_ref, len_ref, pos_ref, neg_ref, qx_ref, px_ref):
    qx_ref[:QR, :] = q_ref[...]
    px_ref[: 2 * SLOTS, :] = p_ref[...]
    lane = lax.broadcasted_iota(jnp.int32, (META, W), 1) // QT
    row = lax.broadcasted_iota(jnp.int32, (META, W), 0)
    acc = jnp.zeros((META, W), jnp.int32)
    per = W // QT
    for q in range(QN):
        here = lane == q % per
        acc = jnp.where(here & (row == q // per), pos_ref[q], acc)
        for a in range(4):
            code = (neg_ref[q, a] // (2 * X * Y * C)) * 2 + neg_ref[q, a] % 2
            acc = jnp.where(here & (row == 2 + 2 * a + q // per), code, acc)
    qx_ref[QR:, :] = acc.astype(F32).astype(BF16)
    acc = jnp.zeros((META, W), jnp.int32)
    for j in range(2):
        acc = jnp.where(row == 2 * j, len_ref[j] // 16, acc)
        acc = jnp.where(row == 2 * j + 1, len_ref[j] % 16, acc)
    px_ref[2 * SLOTS :, :] = acc.astype(F32).astype(BF16)


def pack(q, p, lengths, pos, neg):
    smem = pl.BlockSpec(memory_space=pltpu.SMEM)
    return call(
        pack_body,
        [((QR + META, W), BF16), ((2 * SLOTS + META, W), BF16)],
        [whole((QR, W)), whole((2 * SLOTS, W)), smem, smem, smem],
        name="pack", moved=2**20,
    )(q, p, lengths, pos, neg)


def forward_body(qa_ref, qb_ref, p_ref, meta_ref, e_ref, u_ref, st_ref):
    j = pl.program_id(0)
    p = p_ref[...]
    meta = meta_ref[...].astype(F32)
    length = jnp.where(j == 0, meta[0:1] * 16 + meta[1:2], meta[2:3] * 16 + meta[3:4])
    slot = lax.broadcasted_iota(jnp.int32, (SLOTS, W), 0).astype(F32)
    bias = jnp.where(slot < length, 0.0, LOW).astype(BF16)
    wide = jnp.concatenate([p, bias], axis=1)
    turned = jnp.concatenate([p.astype(F32).T, jnp.ones((16, SLOTS), F32)], axis=0).astype(BF16)
    pick = (lax.broadcasted_iota(jnp.int32, (QR, W), 1) == 0).astype(F32).astype(BF16)
    rows = []
    for k in range(CH):
        ref = qa_ref if k < 4 else qb_ref
        qk = jnp.concatenate([ref[k % 4, :QR, :], pick], axis=1)
        s = lax.dot_general(wide, qk, NT, preferred_element_type=F32)
        top = jnp.max(s, axis=0, keepdims=True)
        e = jnp.exp2((s - top) * SCALE).astype(BF16)
        e_ref[0, :, k * QR : (k + 1) * QR] = e
        u = jnp.dot(turned, e, preferred_element_type=F32)
        total = u[W : W + 1]
        inverse = 1.0 / total
        u_ref[0, k] = (u[:W] * inverse).astype(BF16)
        st_ref[0, 1, k : k + 1, :] = inverse
        rows.append(top + TEMP * jnp.log(total))
    both = jnp.concatenate([r[:, :W] for r in rows] + [r[:, W:] for r in rows], axis=0)
    same = (
        lax.broadcasted_iota(jnp.int32, (W, W), 0) // QT == lax.broadcasted_iota(jnp.int32, (W, W), 1) // QT
    ).astype(F32)
    score = jnp.dot(both, same, preferred_element_type=F32, precision=lax.Precision.HIGHEST)
    st_ref[0, 0, :, :W] = score[:CH]
    st_ref[0, 0, :, W:] = score[CH:]


def forward(qa, qb, px, name):
    return call(
        forward_body,
        [((2, SLOTS, CH * QR), BF16), ((2, CH, W, QR), BF16), ((2, 2, CH, QR), F32)],
        [
            whole((4, QR + META, W)), whole((4, QR + META, W)),
            pl.BlockSpec((SLOTS, W), lambda j: (j, 0)),
            pl.BlockSpec((META, W), lambda j: (2 * SLOTS // META, 0)),
        ],
        [
            pl.BlockSpec((1, SLOTS, CH * QR), lambda j: (j, 0, 0)),
            pl.BlockSpec((1, CH, W, QR), lambda j: (j, 0, 0, 0)),
            pl.BlockSpec((1, 2, CH, QR), lambda j: (j, 0, 0, 0)),
        ],
        grid=(2,), name=name,
        flops=4 * 2 * SLOTS * CH * QR * W * 2, moved=7 * 2**20, exps=2 * SLOTS * CH * QR,
    )(qa, qb, px, px)


META_SPEC = whole((4, META, W), (0, QR // META, 0))


def meta_rows(ma_ref, mb_ref, first):
    rows = []
    for ref in (ma_ref, mb_ref):
        for i in range(4):
            m = ref[i].astype(F32)
            rows.append(jnp.concatenate([m[first : first + 1], m[first + 1 : first + 2]], axis=1))
    return jnp.concatenate(rows, axis=0)


def group_index(dy, j):
    f = lax.axis_index("fsdp")
    x, y, c = f // (Y * C), f // C % Y, f % C
    return (((x * Y + (y + Y - dy) % Y) * C + c) * 2 + j).astype(F32)


def chosen(ma_ref, mb_ref, j):
    code = (lax.axis_index("dp") * 2 + j).astype(F32)
    hit = meta_rows(ma_ref, mb_ref, 2) == code
    for a in range(1, 4):
        hit = hit | (meta_rows(ma_ref, mb_ref, 2 + 2 * a) == code)
    return hit


def negatives_body(st_ref, u_ref, ma_ref, mb_ref, *outs):
    stat_refs, sum_refs = outs[:7], outs[7:]
    hits = [chosen(ma_ref, mb_ref, j) for j in range(2)]
    scores = [jnp.where(hits[j], st_ref[j, 0], LOW) for j in range(2)]
    top = jnp.maximum(scores[0], scores[1])
    weights = [jnp.where(hits[j], jnp.exp(scores[j] - top), 0.0) for j in range(2)]
    total = weights[0] + weights[1]
    for i in range(1, CH):
        for r, v in enumerate((top, total)):
            stat_refs[i - 1][2 * r : 2 * r + 1, :] = v[i : i + 1, :W]
            stat_refs[i - 1][2 * r + 1 : 2 * r + 2, :] = v[i : i + 1, W:]
        sum_refs[i - 1][...] = (
            weights[0][i : i + 1] * u_ref[0, i].astype(F32) + weights[1][i : i + 1] * u_ref[1, i].astype(F32)
        ).astype(BF16)


def negatives(st, u, za, zb):
    out = call(
        negatives_body,
        [((4, W), F32)] * 7 + [((W, QR), BF16)] * 7,
        [whole((2, 2, CH, QR)), whole((2, CH, W, QR)), META_SPEC, META_SPEC],
        name="negatives", flops=2**20, moved=2**21,
    )(st, u, za, zb)
    return out[:7], out[7:]


def stat_row(ref, r):
    return jnp.concatenate([ref[2 * r : 2 * r + 1, :], ref[2 * r + 1 : 2 * r + 2, :]], axis=1)


def local_body(*refs):
    st_refs, ma_ref, mb_ref, neg_refs, out_ref = refs[:4], refs[4], refs[5], refs[6:13], refs[13]
    scores = [st_refs[d][j, 0] for d in range(4) for j in range(2)]
    gids = [group_index(d, j) for d in range(4) for j in range(2)]
    pos = meta_rows(ma_ref, mb_ref, 0)
    top = functools.reduce(jnp.maximum, scores)
    total = sum(jnp.exp(s - top) for s in scores)
    hot = sum(jnp.where(pos == g, s, 0.0) for s, g in zip(scores, gids))
    tops = [stat_row(r, 0) for r in neg_refs]
    sums = [stat_row(r, 1) for r in neg_refs]
    top_n = functools.reduce(jnp.maximum, tops)
    total_n = sum(s * jnp.exp(t - top_n) for s, t in zip(sums, tops))
    new = jnp.maximum(top[:1], top_n)
    first = total[:1] * jnp.exp(top[:1] - new) + total_n * jnp.exp(top_n - new)
    out_ref[:, :QR] = jnp.concatenate([new, top[1:]], axis=0)
    out_ref[:, QR : 2 * QR] = jnp.concatenate([first, total[1:]], axis=0)
    out_ref[:, 2 * QR :] = hot


def local(stats, qa, qb, neg):
    return call(
        local_body, [((CH, 3 * QR), F32)],
        [whole((2, 2, CH, QR))] * 4 + [META_SPEC] * 2 + [whole((4, W))] * 7,
        name="local", flops=2**20, moved=2**18,
    )(*stats, qa, qb, *neg)[0]


def merge(parts):
    top = functools.reduce(jnp.maximum, [p[:, :QR] for p in parts])
    total = sum(p[:, QR : 2 * QR] * jnp.exp(p[:, :QR] - top) for p in parts)
    return top, total, sum(p[:, 2 * QR :] for p in parts)


def cores_body(a_ref, b_ref, out_ref):
    a, b = a_ref[...], b_ref[...]
    parts = merge([a, jnp.concatenate([b[4:], b[:4]], axis=0)])
    for i, v in enumerate(parts):
        out_ref[:, i * QR : (i + 1) * QR] = v


def cores(a, b):
    return call(
        cores_body, [((CH, 3 * QR), F32)], [whole((CH, 3 * QR))] * 2, name="cores", flops=2**16, moved=2**17
    )(a, b)[0]


def line_rows(refs):
    parts = []
    for dx, ref in enumerate(refs):
        v = ref[...]
        order = [(r - dx) % X + h for h in (0, 4) for r in range(4)]
        parts.append(jnp.concatenate([v[o : o + 1] for o in order], axis=0) if dx else v)
    top, total, hot = merge(parts)
    return top + jnp.log(total), hot


def slopes(lse, st_refs, ma_ref, mb_ref):
    pos = meta_rows(ma_ref, mb_ref, 0)
    return [
        jnp.exp(st_refs[d][j, 0] - lse) - (pos == group_index(d, j)).astype(F32)
        for d in range(4) for j in range(2)
    ]


def query_side(slope, u_refs, k, row):
    acc = None
    for i, s in enumerate(slope):
        term = s[row : row + 1] * u_refs[i // 2][i % 2, k].astype(F32)
        acc = term if acc is None else acc + term
    return acc


def far_body(*refs):
    ms, st, u, ma_ref, mb_ref = refs[:4], refs[4:8], refs[8:12], refs[12], refs[13]
    coef_ref, dq_ref, lse_ref, loss_ref = refs[14:]
    lse, hot = line_rows(ms)
    slope = slopes(lse, st, ma_ref, mb_ref)
    for i, s in enumerate(slope):
        coef_ref[i] = s * st[i // 2][i % 2, 1]
    for k in range(4):
        dq_ref[k] = query_side(slope, u, k, 4 + k).astype(BF16)
    for r in range(2):
        lse_ref[r : r + 1, :] = lse[:1, r * W : (r + 1) * W]
        loss_ref[r : r + 1, :] = (lse - hot)[:1, r * W : (r + 1) * W]


def far(ms, st, u, qa, qb):
    return call(
        far_body,
        [((8, CH, QR), F32), ((4, W, QR), BF16), ((2, W), F32), ((2, W), F32)],
        [whole((CH, 3 * QR))] * 4 + [whole((2, 2, CH, QR))] * 4
        + [whole((2, 4, W, QR), (0, 1, 0, 0))] * 4 + [META_SPEC] * 2,
        name="far", flops=2**23, moved=2**21,
    )(*ms, *st, *u, qa, qb)


def near_body(*refs):
    ms, st, u, ma_ref, mb_ref, got_ref = refs[:4], refs[4:8], refs[8:12], refs[12], refs[13], refs[14]
    outs = refs[15:]
    lse, _ = line_rows(ms)
    slope = slopes(lse, st, ma_ref, mb_ref)
    for k in range(4):
        outs[k][...] = (query_side(slope, u, k, k) + got_ref[k].astype(F32)).astype(outs[k].dtype)


def near(ms, st, u, qa, qb, got):
    return call(
        near_body,
        [((W, QR), F32)] + [((W, QR), BF16)] * 3,
        [whole((CH, 3 * QR))] * 4 + [whole((2, 2, CH, QR))] * 4
        + [whole((2, 4, W, QR))] * 4 + [META_SPEC] * 2 + [whole((4, W, QR))],
        name="near", flops=2**23, moved=2**21,
    )(*ms, *st, *u, qa, qb, got)


def turn_body(qa_ref, qb_ref, out_ref):
    for k in range(CH):
        ref = qa_ref if k < 4 else qb_ref
        out_ref[k] = ref[k % 4, :QR, :].astype(F32).T.astype(BF16)


def turn(qa, qb, name):
    return call(
        turn_body, [((CH, W, QR), BF16)], [whole((4, QR + META, W))] * 2, name=name, flops=2**23, moved=2**20
    )(qa, qb)[0]


def passage_side(e, coef, turned_ref):
    scaled = jnp.concatenate(
        [(turned_ref[k].astype(F32) * coef[k : k + 1]).astype(BF16) for k in range(CH)], axis=1
    )
    return lax.dot_general(e, scaled, NT, preferred_element_type=F32)


def back_body(e_ref, coef_ref, turned_ref, dp_ref):
    dp_ref[0] = passage_side(e_ref[0], coef_ref[0], turned_ref).astype(dp_ref.dtype)


def back(e, coef, turned, d, dtype):
    return call(
        back_body,
        [((2, SLOTS, W), dtype)],
        [
            pl.BlockSpec((1, SLOTS, CH * QR), lambda j: (j, 0, 0)),
            pl.BlockSpec((1, CH, QR), lambda j: (2 * d + j, 0, 0)),
            whole((CH, W, QR)),
        ],
        [pl.BlockSpec((1, SLOTS, W), lambda j: (j, 0, 0))],
        grid=(2,), name=f"back{d}",
        flops=2 * 2 * SLOTS * CH * QR * W, moved=5 * 2**20,
    )(e, coef, turned)[0]


def back_neg_body(e_ref, lse_ref, st_ref, ma_ref, mb_ref, turned_ref, own_ref, dp_ref):
    j = pl.program_id(0)
    lse = jnp.concatenate(
        [jnp.concatenate([lse_ref[i, 0:1], lse_ref[i, 1:2]], axis=1) for i in range(CH)], axis=0
    )
    hit = chosen(ma_ref, mb_ref, j)
    coef = jnp.where(hit, jnp.exp(jnp.where(hit, st_ref[0, 0], LOW) - lse), 0.0) * st_ref[0, 1]
    dp_ref[0] = own_ref[0] + passage_side(e_ref[0], coef, turned_ref)


def back_neg(e, lse, st, za, zb, turned, own):
    return call(
        back_neg_body,
        [((2, SLOTS, W), F32)],
        [
            pl.BlockSpec((1, SLOTS, CH * QR), lambda j: (j, 0, 0)),
            whole((CH, 2, W)),
            pl.BlockSpec((1, 2, CH, QR), lambda j: (j, 0, 0, 0)),
            META_SPEC, META_SPEC, whole((CH, W, QR)),
            pl.BlockSpec((1, SLOTS, W), lambda j: (j, 0, 0)),
        ],
        [pl.BlockSpec((1, SLOTS, W), lambda j: (j, 0, 0))],
        grid=(2,), name="back_neg",
        flops=2 * 2 * SLOTS * CH * QR * W, moved=6 * 2**20,
    )(e, lse, st, za, zb, turned, own)[0]


def query_end_body(*refs):
    own_ref, got, lse_ref, stats, sums, out_ref = refs[0], refs[1:4], refs[4], refs[5:12], refs[12:19], refs[19]
    lse = jnp.concatenate([lse_ref[0:1], lse_ref[1:2]], axis=1)
    acc = own_ref[...]
    for g in got:
        acc = acc + g[...].astype(F32)
    for s, v in zip(stats, sums):
        acc = acc + jnp.exp(stat_row(s, 0) - lse) * v[...].astype(F32)
    out_ref[...] = acc.T.astype(BF16)


def query_end(own, got, lse, stats, sums):
    return call(
        query_end_body, [((QR, W), BF16)],
        [whole((W, QR))] * 4 + [whole((2, W))] + [whole((4, W))] * 7 + [whole((W, QR))] * 7,
        name="query_end", flops=2**20, moved=2**20,
    )(own, *got, lse, *stats, *sums)[0]


def passage_end_body(own_ref, *refs):
    acc = own_ref[...]
    for g in refs[:3]:
        acc = acc + g[...].astype(F32)
    refs[3][...] = acc.astype(BF16)


def passage_end(own, got):
    shape = (2, SLOTS, W)
    return call(
        passage_end_body, [(shape, BF16)], [whole(shape)] * 4, name="passage_end", flops=2**19, moved=2**21
    )(own, *got)[0]


def shards(queries, passages, lengths, pos_ids, neg_ids):
    qx, px = pack(queries.reshape(QR, W), passages.reshape(2 * SLOTS, W), lengths, pos_ids, neg_ids)
    za = jnp.stack([qx, along_z(qx, 4)])
    qa = jnp.stack([qx] + [along(qx, dx=d) for d in (1, 2, 3)])
    qb = along(qa, swap=1)
    pxs = [px] + [along(px, dy=d) for d in (1, 2, 3)]
    za = jnp.concatenate([za, along_z(za, 2)])
    zb = along_z(za, 1)

    parts = [forward(qa, qb, pxs[d], f"forward{d}") for d in (0, 1, 2, 3)]
    es, us, sts = [p[0] for p in parts], [p[1] for p in parts], [p[2] for p in parts]
    turned = turn(qa, qb, "turn")
    e_n, u_n, st_n = forward(za, zb, px, "forward_neg")
    turned_n = turn(za, zb, "turn_neg")

    stats, sums = negatives(st_n, u_n, za, zb)
    stats = [along_z(v, ZORDER[i + 1]) for i, v in enumerate(stats)]
    sums = [along_z(v, ZORDER[i + 1]) for i, v in enumerate(sums)]

    ms = local(sts, qa, qb, stats)
    ms = cores(ms, along(ms, swap=1))
    ms = [ms] + [along(ms, dx=d) for d in (1, 2, 3)]

    coef, dq_far, lse, loss = far(ms, sts, us, qa, qb)
    got = along(dq_far, swap=1)
    lz = jnp.stack([lse, along_z(lse, 4)])
    lz = jnp.concatenate([lz, along_z(lz, 2)])
    lz = jnp.concatenate([lz, along_z(lz, 1)])
    dqs = near(ms, sts, us, qa, qb, got)
    dq_got = [along(dqs[r], dx=X - r) for r in (1, 2, 3)]

    dp_got = [along(back(es[d], coef, turned, d, BF16), dy=Y - d) for d in (2, 1, 3)]
    own = back(es[0], coef, turned, 0, F32)
    own = back_neg(e_n, lz, st_n, za, zb, turned_n, own)
    dq = query_end(dqs[0], dq_got, lse, stats, sums)
    dp = passage_end(own, dp_got)
    return loss.reshape(QN, QT)[:, 0], dq.reshape(QN, QT, W), dp


def solution(mesh):
    rows = P(("dp", "fsdp"))
    return jax.shard_map(
        shards, mesh=mesh, in_specs=(rows,) * 5, out_specs=(rows,) * 3, check_vma=False
    )
```

```python
import functools
import math

import jax
import jax.numpy as jnp
from jax import lax
from jax.experimental import pallas as pl
from jax.experimental.pallas import tpu as pltpu
from jax.sharding import PartitionSpec as P

F32, BF16 = jnp.float32, jnp.bfloat16
X, Y, C, Z = 4, 4, 2, 8
QN, QT, W, SLOTS, META = 8, 32, 128, 512, 16
QR = QN * QT
CH = 8
TEMP = 0.1
SCALE = 1.0 / TEMP * math.log2(math.e)
LOW = -1e30
ZORDER = (0, 4, 2, 6, 1, 5, 3, 7)
LIMIT = 8 * 1024 * 1024
NT = (((1,), (1,)), ((), ()))


def index(x, y, c):
    return ((x % X) * Y + (y % Y)) * C + c


def along(value, dx=0, dy=0, swap=0):
    pairs = [
        (index(x, y, c), index(x + dx, y + dy, c ^ swap))
        for x in range(X) for y in range(Y) for c in range(C)
    ]
    return lax.ppermute(value, "fsdp", pairs)


def along_z(value, flip):
    return lax.ppermute(value, "dp", [(z, z ^ flip) for z in range(Z)])


VMEM = pl.BlockSpec(memory_space=pltpu.VMEM)
ANY = pl.BlockSpec(memory_space=pl.ANY)


def call(body, outs, args, in_specs=None, scratch=(), name=None, flops=0, moved=0, exps=0, after=(), limit=LIMIT):
    n, m = len(args), len(after)

    def kernel(*refs):
        body(*refs[:n], *refs[n + m :])

    return pl.pallas_call(
        kernel,
        out_shape=[jax.ShapeDtypeStruct(s, d) for s, d in outs],
        in_specs=([VMEM] * n if in_specs is None else in_specs) + [ANY] * m,
        out_specs=[VMEM] * len(outs),
        scratch_shapes=list(scratch),
        compiler_params=pltpu.CompilerParams(vmem_limit_bytes=limit),
        cost_estimate=pl.CostEstimate(flops=flops, bytes_accessed=moved, transcendentals=exps),
        name=name,
    )(*args, *after)


def pack_body(
    q_ref, p_ref, len_hbm, pos_hbm, neg_hbm, qx_ref, px_ref, len_ref, pos_ref, neg_ref, sems
):
    copies = [
        pltpu.make_async_copy(len_hbm, len_ref, sems.at[0]),
        pltpu.make_async_copy(pos_hbm, pos_ref, sems.at[1]),
        pltpu.make_async_copy(neg_hbm, neg_ref, sems.at[2]),
        pltpu.make_async_copy(q_ref, qx_ref.at[pl.ds(0, QR)], sems.at[3]),
        pltpu.make_async_copy(p_ref, px_ref.at[pl.ds(0, 2 * SLOTS)], sems.at[4]),
    ]
    for c in copies:
        c.start()
    for c in copies[:4]:
        c.wait()
    lane = lax.broadcasted_iota(jnp.int32, (META, W), 1) // QT
    row = lax.broadcasted_iota(jnp.int32, (META, W), 0)
    acc = jnp.zeros((META, W), jnp.int32)
    per = W // QT
    for q in range(QN):
        here = lane == q % per
        acc = jnp.where(here & (row == q // per), pos_ref[q], acc)
        for a in range(4):
            code = (neg_ref[a, q] // (2 * X * Y * C)) * 2 + neg_ref[a, q] % 2
            acc = jnp.where(here & (row == 2 + 2 * a + q // per), code, acc)
    qx_ref[QR:, :] = acc.astype(F32).astype(BF16)
    acc = jnp.zeros((META, W), jnp.int32)
    for j in range(2):
        acc = jnp.where(row == 2 * j, len_ref[j] // 16, acc)
        acc = jnp.where(row == 2 * j + 1, len_ref[j] % 16, acc)
    px_ref[2 * SLOTS :, :] = acc.astype(F32).astype(BF16)
    copies[4].wait()


def pack(q, p, lengths, pos, neg):
    return call(
        pack_body,
        [((QR + META, W), BF16), ((2 * SLOTS + META, W), BF16)],
        (q, p, lengths, pos, neg.T), [ANY] * 5,
        [
            pltpu.SMEM((2,), jnp.int32), pltpu.SMEM((QN,), jnp.int32), pltpu.SMEM((4, QN), jnp.int32),
            pltpu.SemaphoreType.DMA((5,)),
        ],
        name="pack", moved=2**20, limit=63_143_936,
    )


def stack_body(*refs):
    at = 0
    for ref in refs[:-1]:
        n = ref.shape[0] if ref.ndim == 3 else 1
        refs[-1][at : at + n] = ref[...].reshape(n, *ref.shape[-2:])
        at += n


def stack(parts, name, after=()):
    n = sum(p.shape[0] if p.ndim == 3 else 1 for p in parts)
    return call(stack_body, [((n, *parts[0].shape[-2:]), parts[0].dtype)], parts, name=name, moved=2**19, after=after)[0]


def forward_body(*refs):
    q_refs, (p_ref, e_ref, u_ref, st_ref) = refs[:-4], refs[-4:]
    q_at = [(r, i) for r in q_refs for i in range(r.shape[0])]
    meta = p_ref[2 * SLOTS :, :].astype(F32)
    slot = lax.broadcasted_iota(jnp.int32, (SLOTS, W), 0).astype(F32)
    pick = (lax.broadcasted_iota(jnp.int32, (QR, W), 1) == 0).astype(F32).astype(BF16)
    wide, turned = [], []
    for j in range(2):
        p = p_ref[j * SLOTS : (j + 1) * SLOTS, :]
        length = meta[2 * j : 2 * j + 1] * 16 + meta[2 * j + 1 : 2 * j + 2]
        bias = jnp.where(slot < length, 0.0, LOW).astype(BF16)
        wide.append(jnp.concatenate([p, bias], axis=1))
        turned.append(jnp.concatenate([p.astype(F32).T, jnp.ones((16, SLOTS), F32)], axis=0).astype(BF16))
    rows = [[None] * CH for _ in range(2)]

    def product(j, k):
        ref, i = q_at[k]
        qk = jnp.concatenate([ref[i, :QR, :], pick], axis=1)
        return lax.dot_general(wide[j], qk, NT, preferred_element_type=F32)

    def finish(j, k, top, e):
        u = jnp.dot(turned[j], e, preferred_element_type=F32)
        total = u[W : W + 1]
        inverse = 1.0 / total
        u_ref[j, k] = (u[:W] * inverse).astype(BF16)
        st_ref[j, 1, k : k + 1, :] = inverse
        rows[j][k] = top + TEMP * jnp.log(total)

    tiles = [(j, k) for j in range(2) for k in range(CH)]
    s, waiting = product(*tiles[0]), []
    for i, (j, k) in enumerate(tiles):
        later = product(*tiles[i + 1]) if i + 1 < len(tiles) else None
        top = jnp.max(s, axis=0, keepdims=True)
        e = jnp.exp2(s * SCALE - top * SCALE).astype(BF16)
        e_ref[j, :, k * QR : (k + 1) * QR] = e
        waiting.append((j, k, top, e))
        if len(waiting) > 2:
            finish(*waiting.pop(0))
        s = later
    for w in waiting:
        finish(*w)
    same = (
        lax.broadcasted_iota(jnp.int32, (W, W), 0) // QT == lax.broadcasted_iota(jnp.int32, (W, W), 1) // QT
    ).astype(F32)
    both = jnp.concatenate([r[:, h * W : (h + 1) * W] for j in range(2) for h in range(2) for r in rows[j]], axis=0)
    score = jnp.dot(both, same, preferred_element_type=F32, precision=lax.Precision.HIGHEST)
    for j in range(2):
        for h in range(2):
            st_ref[j, 0, :, h * W : (h + 1) * W] = score[(2 * j + h) * CH : (2 * j + h + 1) * CH]


def forward(qs, px, name, after=()):
    return call(
        forward_body,
        [((2, SLOTS, CH * QR), BF16), ((2, CH, W, QR), BF16), ((2, 2, CH, QR), F32)],
        (*qs, px), name=name,
        flops=4 * 2 * SLOTS * CH * QR * W * 2, moved=7 * 2**20, exps=2 * SLOTS * CH * QR, after=after,
    )


def meta_rows(q_refs, first):
    rows = []
    for ref in q_refs:
        for i in range(ref.shape[0]):
            m = ref[i, QR:, :].astype(F32)
            rows.append(jnp.concatenate([m[first : first + 1], m[first + 1 : first + 2]], axis=1))
    return jnp.concatenate(rows, axis=0)


def group_index(dy, j):
    f = lax.axis_index("fsdp")
    x, y, c = f // (Y * C), f // C % Y, f % C
    return (((x * Y + (y + Y - dy) % Y) * C + c) * 2 + j).astype(F32)


def chosen(z_refs, j):
    code = (lax.axis_index("dp") * 2 + j).astype(F32)
    hit = meta_rows(z_refs, 2) == code
    for a in range(1, 4):
        hit = hit | (meta_rows(z_refs, 2 + 2 * a) == code)
    return hit


def chosen_scores(st_ref, z_refs):
    hits = [chosen(z_refs, j) for j in range(2)]
    return hits, [jnp.where(hits[j], st_ref[j, 0], LOW) for j in range(2)]


def neg_stats_body(st_ref, za_ref, zb_ref, out_ref):
    hits, scores = chosen_scores(st_ref, (za_ref, zb_ref))
    top = jnp.maximum(scores[0], scores[1])
    out_ref[:, :QR] = top
    out_ref[:, QR:] = sum(jnp.where(h, jnp.exp(s - top), 0.0) for h, s in zip(hits, scores))


def neg_stats(st, zs):
    return call(neg_stats_body, [((Z, 2 * QR), F32)], (st, *zs), name="neg_stats", flops=2**16, moved=2**17)[0]


def pair(a, b, flip):
    rows = [ZORDER.index(d ^ flip) for d in ZORDER]
    b = jnp.concatenate([b[r : r + 1] for r in rows], axis=0)
    top = jnp.maximum(a[:, :QR], b[:, :QR])
    return top, a[:, QR:] * jnp.exp(a[:, :QR] - top) + b[:, QR:] * jnp.exp(b[:, :QR] - top)


def pair_body(a_ref, b_ref, out_ref, *, flip):
    out_ref[:, :QR], out_ref[:, QR:] = pair(a_ref[...], b_ref[...], flip)


def pair_up(a, flip, after):
    return call(
        functools.partial(pair_body, flip=flip), [((Z, 2 * QR), F32)], (a, along_z(a, flip)), name=f"pair{flip}",
        flops=2**16, moved=2**16, after=[after],
    )[0]


def split3(v):
    high = v.astype(BF16)
    rest = v - high.astype(F32)
    middle = rest.astype(BF16)
    return [high.astype(F32), middle.astype(F32), rest - middle.astype(F32)]


def put_rows(ref, rows):
    rows = jnp.concatenate([*rows, jnp.zeros((META - len(rows), QR), F32)], axis=0)
    ref[ref.shape[0] - META :, :] = rows.astype(BF16)


def get_rows(ref, n):
    tail = ref[ref.shape[0] - META :, :].astype(F32)
    return [tail[i : i + 1] for i in range(n)]


def neg_sums_body(st_ref, u_ref, za_ref, zb_ref, a_ref, b_ref, lse_ref, top_ref, send_ref, keep_ref):
    top, _ = pair(a_ref[...], b_ref[...], 1)
    top_ref[...] = top[:1]
    hits, scores = chosen_scores(st_ref, (za_ref, zb_ref))
    w = [jnp.where(h, jnp.exp(s - top), 0.0) for h, s in zip(hits, scores)]
    for n, d in enumerate((0, 2, 4, 6)):
        for ref, i in ((keep_ref, ZORDER.index(d)), (send_ref, ZORDER.index(d + 1))):
            ref[n * W : (n + 1) * W, :] = (
                w[0][i : i + 1] * u_ref[0, i].astype(F32) + w[1][i : i + 1] * u_ref[1, i].astype(F32)
            ).astype(BF16)
    put_rows(send_ref, split3(lse_ref[0]))


def neg_sums(st, u, zs, a, b, lse):
    return call(
        neg_sums_body, [((1, QR), F32), ((4 * W + META, QR), BF16), ((4 * W, QR), BF16)], (st, u, *zs, a, b, lse),
        name="neg_sums", flops=2**20, moved=2**21,
    )


def halve_body(keep_ref, sent_ref, got_ref, send_out, keep_out):
    n = keep_out.shape[0] // W
    for i in range(n):
        for ref, k in ((keep_out, 2 * i), (send_out, 2 * i + 1)):
            at = slice(k * W, (k + 1) * W)
            ref[i * W : (i + 1) * W, :] = (keep_ref[at, :].astype(F32) + got_ref[at, :].astype(F32)).astype(BF16)
    known = 3 * 2 // n
    put_rows(send_out, get_rows(sent_ref, known) + get_rows(got_ref, known))


def halve(keep, sent, got, name, after=()):
    n = keep.shape[0] // 2
    return call(
        halve_body, [((n + META, QR), BF16), ((n, QR), BF16)], (keep, sent, got), name=name, flops=2**18, moved=2**20,
        after=after,
    )


def local_body(*refs):
    st_refs, q_refs, a_ref, b_ref, out_ref = refs[:4], refs[4:6], refs[6], refs[7], refs[8]
    scores = [st_refs[d][j, 0] for d in range(4) for j in range(2)]
    gids = [group_index(d, j) for d in range(4) for j in range(2)]
    pos = meta_rows(q_refs, 0)
    top = functools.reduce(jnp.maximum, scores)
    total = sum(jnp.exp(s - top) for s in scores)
    hot = sum(jnp.where(pos == g, s, 0.0) for s, g in zip(scores, gids))
    top_n, total_n = (v[:1] for v in pair(a_ref[...], b_ref[...], 1))
    new = jnp.maximum(top[:1], top_n)
    first = total[:1] * jnp.exp(top[:1] - new) + total_n * jnp.exp(top_n - new)
    out_ref[:, :QR] = jnp.concatenate([new, top[1:]], axis=0)
    out_ref[:, QR : 2 * QR] = jnp.concatenate([first, total[1:]], axis=0)
    out_ref[:, 2 * QR :] = hot


def local(stats, qs, a, b):
    return call(local_body, [((CH, 3 * QR), F32)], (*stats, *qs, a, b), name="local", flops=2**20, moved=2**18)[0]


def merge(parts):
    top = functools.reduce(jnp.maximum, [p[:, :QR] for p in parts])
    total = sum(p[:, QR : 2 * QR] * jnp.exp(p[:, :QR] - top) for p in parts)
    return top, total, sum(p[:, 2 * QR :] for p in parts)


def cores_body(a_ref, b_ref, out_ref):
    a, b = a_ref[...], b_ref[...]
    parts = merge([a, jnp.concatenate([b[4:], b[:4]], axis=0)])
    for i, v in enumerate(parts):
        out_ref[:, i * QR : (i + 1) * QR] = v


def cores(a, b):
    return call(cores_body, [((CH, 3 * QR), F32)], (a, b), name="cores", flops=2**16, moved=2**17)[0]


def line_rows(refs):
    parts = []
    for dx, ref in enumerate(refs):
        v = ref[...]
        order = [(r - dx) % X + h for h in (0, 4) for r in range(4)]
        parts.append(jnp.concatenate([v[o : o + 1] for o in order], axis=0) if dx else v)
    top, total, hot = merge(parts)
    return top + jnp.log(total), hot


def slopes(lse, st_refs, q_refs):
    pos = meta_rows(q_refs, 0)
    return [
        jnp.exp(st_refs[d][j, 0] - lse) - (pos == group_index(d, j)).astype(F32)
        for d in range(4) for j in range(2)
    ]


def query_side(slope, u_refs, k, row):
    acc = None
    for i, s in enumerate(slope):
        term = s[row : row + 1] * u_refs[i // 2][i % 2, k].astype(F32)
        acc = term if acc is None else acc + term
    return acc


def far_body(*refs):
    ms, st, u, q_refs = refs[:4], refs[4:8], refs[8:12], refs[12:14]
    coef_ref, dq_ref, lse_ref, loss_ref = refs[14:]
    lse, hot = line_rows(ms)
    slope = slopes(lse, st, q_refs)
    for i, s in enumerate(slope):
        coef_ref[i] = s * st[i // 2][i % 2, 1]
    for k in range(4):
        dq_ref[k] = query_side(slope, u, 4 + k, 4 + k).astype(BF16)
    lse_ref[0] = lse[:1]
    at = lax.broadcasted_iota(jnp.int32, (QR, QN), 0) == QT * lax.broadcasted_iota(jnp.int32, (QR, QN), 1)
    loss_ref[...] = jnp.dot(
        (lse - hot)[:1], at.astype(F32), preferred_element_type=F32, precision=lax.Precision.HIGHEST
    )


def far(ms, st, u, qs, after=()):
    return call(
        far_body,
        [((8, CH, QR), F32), ((4, W, QR), BF16), ((1, 1, QR), F32), ((1, QN), F32)],
        (*ms, *st, *u, *qs), name="far", flops=2**23, moved=2**21, after=after,
    )


def near_body(*refs):
    ms, st, u, q_refs, got_ref, outs = refs[:4], refs[4:8], refs[8:12], refs[12:14], refs[14], refs[15:]
    lse, _ = line_rows(ms)
    slope = slopes(lse, st, q_refs)
    for k in range(4):
        outs[k][...] = (query_side(slope, u, k, k) + got_ref[k].astype(F32)).astype(outs[k].dtype)


def near(ms, st, u, qs, got):
    return call(
        near_body, [((W, QR), F32)] + [((W, QR), BF16)] * 3,
        (*ms, *st, *u, *qs, got), name="near", flops=2**23, moved=2**21,
    )


def turn_body(*refs):
    k = 0
    for ref in refs[:-1]:
        for i in range(ref.shape[0]):
            refs[-1][k] = ref[i, :QR, :].astype(F32).T.astype(BF16)
            k += 1


def turn(qs, name):
    return call(turn_body, [((CH, W, QR), BF16)], qs, name=name, flops=2**23, moved=2**20)[0]


def passage_side(e, coef, turned_ref):
    scaled = jnp.concatenate(
        [(turned_ref[k].astype(F32) * coef[k : k + 1]).astype(BF16) for k in range(CH)], axis=1
    )
    return lax.dot_general(e, scaled, NT, preferred_element_type=F32)


def back_body(e_ref, coef_ref, turned_ref, dp_ref, *, d):
    for j in range(2):
        dp_ref[j] = passage_side(e_ref[j], coef_ref[2 * d + j], turned_ref).astype(dp_ref.dtype)


def back(e, coef, turned, d, dtype, after=()):
    return call(
        functools.partial(back_body, d=d), [((2, SLOTS, W), dtype)], (e, coef, turned), name=f"back{d}",
        flops=2 * 2 * SLOTS * CH * QR * W, moved=5 * 2**20, after=after,
    )[0]


def back_neg_body(e_ref, sent_ref, got_ref, st_ref, za_ref, zb_ref, turned_ref, own_ref, dp_ref):
    rows = get_rows(sent_ref, 12) + get_rows(got_ref, 12)
    lse = jnp.concatenate([rows[3 * d] + rows[3 * d + 1] + rows[3 * d + 2] for d in ZORDER], axis=0)
    for j in range(2):
        hit = chosen((za_ref, zb_ref), j)
        coef = jnp.where(hit, jnp.exp(jnp.where(hit, st_ref[j, 0], LOW) - lse), 0.0) * st_ref[j, 1]
        dp_ref[j] = own_ref[j] + passage_side(e_ref[j], coef, turned_ref)


def back_neg(e, sent, got, st, zs, turned, own):
    return call(
        back_neg_body, [((2, SLOTS, W), F32)], (e, sent, got, st, *zs, turned, own), name="back_neg",
        flops=2 * 2 * SLOTS * CH * QR * W, moved=6 * 2**20,
    )[0]


def end_body(own_ref, g1, g2, g3, lse_ref, top_ref, n1, n2, dp_ref, p1, p2, p3, dq_out, dp_out):
    acc = own_ref[...]
    for g in (g1, g2, g3):
        acc = acc + g[...].astype(F32)
    acc = acc + jnp.exp(top_ref[...] - lse_ref[0]) * (n1[...].astype(F32) + n2[:W, :].astype(F32))
    dq_out[...] = acc.T.astype(BF16)
    acc = dp_ref[...]
    for g in (p1, p2, p3):
        acc = acc + g[...].astype(F32)
    dp_out[...] = acc.astype(BF16)


def end(own, got, lse, top, sums, dp, dp_got):
    return call(
        end_body, [((QR, W), BF16), ((2, SLOTS, W), BF16)], (own, *got, lse, top, *sums, dp, *dp_got), name="end",
        flops=2**20, moved=2**21,
    )


def shards(queries, passages, lengths, pos_ids, neg_ids):
    qx, px = pack(queries.reshape(QR, W), passages.reshape(2 * SLOTS, W), lengths, pos_ids, neg_ids)
    z2 = stack([qx, along_z(qx, 4)], "stack_z2")
    qa = stack([qx] + [along(qx, dx=d) for d in (1, 2, 3)], "stack_x", after=[z2])
    qs = (qa, along(qa, swap=1))
    pxs = [px] + [along(px, dy=d) for d in (1, 2, 3)]
    parts = [forward(qs, pxs[0], "forward0")]
    z4 = stack([z2, along_z(z2, 2)], "stack_z4", after=[parts[0][2]])
    zs = (z4, along_z(z4, 1))
    parts.append(forward(qs, pxs[1], "forward1", after=[z4]))
    e_n, u_n, st_n = forward(zs, px, "forward_neg", after=[parts[1][2]])
    neg = neg_stats(st_n, zs)
    parts.append(forward(qs, pxs[2], "forward2", after=[neg]))
    neg = pair_up(neg, 4, parts[2][2])
    parts.append(forward(qs, pxs[3], "forward3", after=[neg]))
    neg = pair_up(neg, 2, parts[3][2])
    negs = (neg, along_z(neg, 1))
    es, us, sts = [p[0] for p in parts], [p[1] for p in parts], [p[2] for p in parts]
    turned, turned_n = turn(qs, "turn"), turn(zs, "turn_neg")

    ms = local(sts, qs, *negs)
    ms = cores(ms, along(ms, swap=1))
    ms = [ms] + [along(ms, dx=d) for d in (1, 2, 3)]

    coef, dq_far, lse, loss = far(ms, sts, us, qs)
    got = along(dq_far, swap=1)
    top, sent, keep = neg_sums(st_n, u_n, zs, *negs, lse)
    back_got = along_z(sent, 1)
    dp_got = [along(back(es[2], coef, turned, 2, BF16, after=[top]), dy=2)]
    dp_got.append(along(back(es[1], coef, turned, 1, BF16), dy=3))
    dqs = near(ms, sts, us, qs, got)
    sent, keep = halve(keep, sent, back_got, "halve4")
    back_got = along_z(sent, 2)
    dp_got.append(along(back(es[3], coef, turned, 3, BF16, after=[dqs[0], keep]), dy=1))
    dq_got = [along(dqs[r], dx=X - r) for r in (1, 2, 3)]
    own = back(es[0], coef, turned, 0, F32)
    sent, keep = halve(keep, sent, back_got, "halve2")
    back_got = along_z(sent, 4)
    own = back_neg(e_n, sent, back_got, st_n, zs, turned_n, own)
    dq, dp = end(dqs[0], dq_got, lse, top, (keep, back_got), own, dp_got)
    return loss.reshape(QN), dq.reshape(QN, QT, W), dp


def solution(mesh):
    rows = P(("dp", "fsdp"))
    return jax.shard_map(
        shards, mesh=mesh, in_specs=(rows,) * 5, out_specs=(rows,) * 3, check_vma=False
    )
```

```python
import functools
import math

import jax
import jax.numpy as jnp
from jax import lax
from jax.experimental import pallas as pl
from jax.experimental.pallas import tpu as pltpu
from jax.sharding import PartitionSpec as P

F32, BF16 = jnp.float32, jnp.bfloat16
X, Y, C, Z = 4, 4, 2, 8
QN, QT, W, SLOTS, META = 8, 32, 128, 512, 16
QR = QN * QT
CH = 8
TEMP = 0.1
SCALE = 1.0 / TEMP * math.log2(math.e)
LOW = -1e30
ZORDER = (0, 4, 2, 6, 1, 5, 3, 7)
LIMIT = 8 * 1024 * 1024
NT = (((1,), (1,)), ((), ()))


def index(x, y, c):
    return ((x % X) * Y + (y % Y)) * C + c


def along(value, dx=0, dy=0, swap=0):
    pairs = [
        (index(x, y, c), index(x + dx, y + dy, c ^ swap))
        for x in range(X) for y in range(Y) for c in range(C)
    ]
    return lax.ppermute(value, "fsdp", pairs)


def along_z(value, flip):
    return lax.ppermute(value, "dp", [(z, z ^ flip) for z in range(Z)])


VMEM = pl.BlockSpec(memory_space=pltpu.VMEM)
ANY = pl.BlockSpec(memory_space=pl.ANY)


def call(body, outs, args, in_specs=None, scratch=(), name=None, flops=0, moved=0, exps=0, after=(), limit=LIMIT):
    n, m = len(args), len(after)

    def kernel(*refs):
        body(*refs[:n], *refs[n + m :])

    return pl.pallas_call(
        kernel,
        out_shape=[jax.ShapeDtypeStruct(s, d) for s, d in outs],
        in_specs=([VMEM] * n if in_specs is None else in_specs) + [ANY] * m,
        out_specs=[VMEM] * len(outs),
        scratch_shapes=list(scratch),
        compiler_params=pltpu.CompilerParams(vmem_limit_bytes=limit),
        cost_estimate=pl.CostEstimate(flops=flops, bytes_accessed=moved, transcendentals=exps),
        name=name,
    )(*args, *after)


def pack_body(
    q_ref, p_ref, len_hbm, pos_hbm, neg_hbm, qx_ref, px_ref, len_ref, pos_ref, neg_ref, sems
):
    copies = [
        pltpu.make_async_copy(len_hbm, len_ref, sems.at[0]),
        pltpu.make_async_copy(pos_hbm, pos_ref, sems.at[1]),
        pltpu.make_async_copy(neg_hbm, neg_ref, sems.at[2]),
        pltpu.make_async_copy(q_ref, qx_ref.at[pl.ds(0, QR)], sems.at[3]),
        pltpu.make_async_copy(p_ref, px_ref.at[pl.ds(0, 2 * SLOTS)], sems.at[4]),
    ]
    for c in copies:
        c.start()
    for c in copies[:4]:
        c.wait()
    lane = lax.broadcasted_iota(jnp.int32, (META, W), 1) // QT
    row = lax.broadcasted_iota(jnp.int32, (META, W), 0)
    acc = jnp.zeros((META, W), jnp.int32)
    per = W // QT
    for q in range(QN):
        here = lane == q % per
        acc = jnp.where(here & (row == q // per), pos_ref[q], acc)
        for a in range(4):
            code = (neg_ref[a, q] // (2 * X * Y * C)) * 2 + neg_ref[a, q] % 2
            acc = jnp.where(here & (row == 2 + 2 * a + q // per), code, acc)
    qx_ref[QR:, :] = acc.astype(F32).astype(BF16)
    acc = jnp.zeros((META, W), jnp.int32)
    for j in range(2):
        acc = jnp.where(row == 2 * j, len_ref[j] // 16, acc)
        acc = jnp.where(row == 2 * j + 1, len_ref[j] % 16, acc)
    px_ref[2 * SLOTS :, :] = acc.astype(F32).astype(BF16)
    copies[4].wait()


def pack(q, p, lengths, pos, neg):
    return call(
        pack_body,
        [((QR + META, W), BF16), ((2 * SLOTS + META, W), BF16)],
        (q, p, lengths, pos, neg.T), [ANY] * 5,
        [
            pltpu.SMEM((2,), jnp.int32), pltpu.SMEM((QN,), jnp.int32), pltpu.SMEM((4, QN), jnp.int32),
            pltpu.SemaphoreType.DMA((5,)),
        ],
        name="pack", moved=2**20, limit=63_143_936,
    )


def stack_body(*refs):
    at = 0
    for ref in refs[:-1]:
        n = ref.shape[0] if ref.ndim == 3 else 1
        refs[-1][at : at + n] = ref[...].reshape(n, *ref.shape[-2:])
        at += n


def stack(parts, name, after=()):
    n = sum(p.shape[0] if p.ndim == 3 else 1 for p in parts)
    return call(stack_body, [((n, *parts[0].shape[-2:]), parts[0].dtype)], parts, name=name, moved=2**19, after=after)[0]


def forward_body(*refs, skip):
    q_refs, (p_ref, e_ref, u_ref, st_ref) = refs[:-4], refs[-4:]
    q_at = [(r, i) for r in q_refs for i in range(r.shape[0])][skip:]
    chunks = len(q_at)
    meta = p_ref[2 * SLOTS :, :].astype(F32)
    slot = lax.broadcasted_iota(jnp.int32, (SLOTS, W), 0).astype(F32)
    pick = (lax.broadcasted_iota(jnp.int32, (QR, W), 1) == 0).astype(F32).astype(BF16)
    wide, turned = [], []
    for j in range(2):
        p = p_ref[j * SLOTS : (j + 1) * SLOTS, :]
        length = meta[2 * j : 2 * j + 1] * 16 + meta[2 * j + 1 : 2 * j + 2]
        bias = jnp.where(slot < length, 0.0, LOW).astype(BF16)
        wide.append(jnp.concatenate([p, bias], axis=1))
        turned.append(jnp.concatenate([p.astype(F32).T, jnp.ones((16, SLOTS), F32)], axis=0).astype(BF16))
    rows = [[None] * chunks for _ in range(2)]

    def product(j, k):
        ref, i = q_at[k]
        qk = jnp.concatenate([ref[i, :QR, :], pick], axis=1)
        return lax.dot_general(wide[j], qk, NT, preferred_element_type=F32)

    def finish(j, k, top, e):
        u = jnp.dot(turned[j], e, preferred_element_type=F32)
        total = u[W : W + 1]
        inverse = 1.0 / total
        u_ref[j, k] = (u[:W] * inverse).astype(BF16)
        st_ref[j, 1, k : k + 1, :] = inverse
        rows[j][k] = top + TEMP * jnp.log(total)

    tiles = [(j, k) for j in range(2) for k in range(chunks)]
    s, waiting = product(*tiles[0]), []
    for i, (j, k) in enumerate(tiles):
        later = product(*tiles[i + 1]) if i + 1 < len(tiles) else None
        top = jnp.max(s, axis=0, keepdims=True)
        e = jnp.exp2((s - top) * SCALE).astype(BF16)
        e_ref[j, :, k * QR : (k + 1) * QR] = e
        waiting.append((j, k, top, e))
        if len(waiting) > 2:
            finish(*waiting.pop(0))
        s = later
    for w in waiting:
        finish(*w)
    same = (
        lax.broadcasted_iota(jnp.int32, (W, W), 0) // QT == lax.broadcasted_iota(jnp.int32, (W, W), 1) // QT
    ).astype(F32)
    both = jnp.concatenate([r[:, h * W : (h + 1) * W] for j in range(2) for h in range(2) for r in rows[j]], axis=0)
    score = jnp.dot(both, same, preferred_element_type=F32, precision=lax.Precision.HIGHEST)
    for j in range(2):
        for h in range(2):
            st_ref[j, 0, :, h * W : (h + 1) * W] = score[(2 * j + h) * chunks : (2 * j + h + 1) * chunks]


def forward(qs, px, name, skip=0, after=()):
    chunks = CH - skip
    work = 2 * SLOTS * chunks * QR
    return call(
        functools.partial(forward_body, skip=skip),
        [((2, SLOTS, chunks * QR), BF16), ((2, chunks, W, QR), BF16), ((2, 2, chunks, QR), F32)],
        (*qs, px), name=name, flops=8 * work * W, moved=7 * 2**20, exps=work, after=after,
    )


def meta_rows(q_refs, first):
    rows = []
    for ref in q_refs:
        for i in range(ref.shape[0]):
            m = ref[i, QR:, :].astype(F32)
            rows.append(jnp.concatenate([m[first : first + 1], m[first + 1 : first + 2]], axis=1))
    return jnp.concatenate(rows, axis=0)


def group_index(dy, j):
    f = lax.axis_index("fsdp")
    x, y, c = f // (Y * C), f // C % Y, f % C
    return (((x * Y + (y + Y - dy) % Y) * C + c) * 2 + j).astype(F32)


def chosen(z_refs, j):
    code = (lax.axis_index("dp") * 2 + j).astype(F32)
    hit = meta_rows(z_refs, 2)[1:] == code
    for a in range(1, 4):
        hit = hit | (meta_rows(z_refs, 2 + 2 * a)[1:] == code)
    return hit


def chosen_scores(st_ref, z_refs):
    hits = [chosen(z_refs, j) for j in range(2)]
    return hits, [jnp.where(hits[j], st_ref[j, 0], LOW) for j in range(2)]


def neg_stats_body(st_ref, za_ref, zb_ref, out_ref):
    hits, scores = chosen_scores(st_ref, (za_ref, zb_ref))
    top = jnp.maximum(scores[0], scores[1])
    total = sum(jnp.where(h, jnp.exp(s - top), 0.0) for h, s in zip(hits, scores))
    out_ref[:, :QR] = jnp.concatenate([jnp.full((1, QR), LOW, F32), top], axis=0)
    out_ref[:, QR:] = jnp.concatenate([jnp.zeros((1, QR), F32), total], axis=0)


def neg_stats(st, zs):
    return call(neg_stats_body, [((Z, 2 * QR), F32)], (st, *zs), name="neg_stats", flops=2**16, moved=2**17)[0]


def pair(a, b, flip):
    rows = [ZORDER.index(d ^ flip) for d in ZORDER]
    b = jnp.concatenate([b[r : r + 1] for r in rows], axis=0)
    top = jnp.maximum(a[:, :QR], b[:, :QR])
    return top, a[:, QR:] * jnp.exp(a[:, :QR] - top) + b[:, QR:] * jnp.exp(b[:, :QR] - top)


def pair_body(a_ref, b_ref, out_ref, *, flip):
    out_ref[:, :QR], out_ref[:, QR:] = pair(a_ref[...], b_ref[...], flip)


def pair_up(a, flip, after):
    return call(
        functools.partial(pair_body, flip=flip), [((Z, 2 * QR), F32)], (a, along_z(a, flip)), name=f"pair{flip}",
        flops=2**16, moved=2**16, after=[after],
    )[0]


def split3(v):
    high = v.astype(BF16)
    rest = v - high.astype(F32)
    middle = rest.astype(BF16)
    return [high.astype(F32), middle.astype(F32), rest - middle.astype(F32)]


def put_rows(ref, rows):
    rows = jnp.concatenate([*rows, jnp.zeros((META - len(rows), QR), F32)], axis=0)
    ref[ref.shape[0] - META :, :] = rows.astype(BF16)


def get_rows(ref, n):
    tail = ref[ref.shape[0] - META :, :].astype(F32)
    return [tail[i : i + 1] for i in range(n)]


def neg_sums_body(st_ref, u_ref, za_ref, zb_ref, a_ref, b_ref, top_ref, send_ref, keep_ref):
    top, _ = pair(a_ref[...], b_ref[...], 1)
    top_ref[...] = top[:1]
    hits, scores = chosen_scores(st_ref, (za_ref, zb_ref))
    w = [jnp.where(h, jnp.exp(s - top[1:]), 0.0) for h, s in zip(hits, scores)]
    for n, d in enumerate((0, 2, 4, 6)):
        for ref, i in ((keep_ref, ZORDER.index(d)), (send_ref, ZORDER.index(d + 1))):
            if d or ref is send_ref:
                sums = [w[j][i - 1 : i] * u_ref[j, i - 1].astype(F32) for j in range(2)]
                ref[n * W : (n + 1) * W, :] = (sums[0] + sums[1]).astype(BF16)
            else:
                ref[n * W : (n + 1) * W, :] = jnp.zeros((W, QR), BF16)


def neg_sums(st, u, zs, a, b, after=()):
    return call(
        neg_sums_body, [((1, QR), F32)] + [((4 * W, QR), BF16)] * 2, (st, u, *zs, a, b),
        name="neg_sums", flops=2**20, moved=2**21, after=after,
    )


def halve_body(keep_ref, got_ref, a_ref, b_ref, send_out, keep_out):
    n = keep_out.shape[0] // W
    for i in range(n):
        for ref, k in ((keep_out, 2 * i), (send_out, 2 * i + 1)):
            at = slice(k * W, (k + 1) * W)
            ref[i * W : (i + 1) * W, :] = (keep_ref[at, :].astype(F32) + got_ref[at, :].astype(F32)).astype(BF16)
    if n == 2:
        rows = split3(a_ref[0]) + split3(b_ref[0])
    else:
        rows = get_rows(a_ref, 6) + get_rows(b_ref, 6)
    put_rows(send_out, rows)


def halve(keep, got, a, b, name, after=()):
    n = keep.shape[0] // 2
    return call(
        halve_body, [((n + META, QR), BF16), ((n, QR), BF16)], (keep, got, a, b), name=name, flops=2**18, moved=2**20,
        after=after,
    )


def local_body(*refs):
    st_refs, q_refs, a_ref, b_ref, out_ref = refs[:4], refs[4:6], refs[6], refs[7], refs[8]
    scores = [st_refs[d][j, 0] for d in range(4) for j in range(2)]
    gids = [group_index(d, j) for d in range(4) for j in range(2)]
    pos = meta_rows(q_refs, 0)
    top = functools.reduce(jnp.maximum, scores)
    total = sum(jnp.exp(s - top) for s in scores)
    hot = sum(jnp.where(pos == g, s, 0.0) for s, g in zip(scores, gids))
    top_n, total_n = (v[:1] for v in pair(a_ref[...], b_ref[...], 1))
    new = jnp.maximum(top[:1], top_n)
    first = total[:1] * jnp.exp(top[:1] - new) + total_n * jnp.exp(top_n - new)
    out_ref[:, :QR] = jnp.concatenate([new, top[1:]], axis=0)
    out_ref[:, QR : 2 * QR] = jnp.concatenate([first, total[1:]], axis=0)
    out_ref[:, 2 * QR :] = hot


def local(stats, qs, a, b):
    return call(local_body, [((CH, 3 * QR), F32)], (*stats, *qs, a, b), name="local", flops=2**20, moved=2**18)[0]


def merge(parts):
    top = functools.reduce(jnp.maximum, [p[:, :QR] for p in parts])
    total = sum(p[:, QR : 2 * QR] * jnp.exp(p[:, :QR] - top) for p in parts)
    return top, total, sum(p[:, 2 * QR :] for p in parts)


def cores_body(a_ref, b_ref, out_ref):
    a, b = a_ref[...], b_ref[...]
    parts = merge([a, jnp.concatenate([b[4:], b[:4]], axis=0)])
    for i, v in enumerate(parts):
        out_ref[:, i * QR : (i + 1) * QR] = v


def cores(a, b, after=()):
    return call(cores_body, [((CH, 3 * QR), F32)], (a, b), name="cores", flops=2**16, moved=2**17)[0]


def line_rows(refs):
    parts = []
    for dx, ref in enumerate(refs):
        v = ref[...]
        order = [(r - dx) % X + h for h in (0, 4) for r in range(4)]
        parts.append(jnp.concatenate([v[o : o + 1] for o in order], axis=0) if dx else v)
    top, total, hot = merge(parts)
    return top + jnp.log(total), hot


def slopes(lse, st_refs, q_refs):
    pos = meta_rows(q_refs, 0)
    return [
        jnp.exp(st_refs[d][j, 0] - lse) - (pos == group_index(d, j)).astype(F32)
        for d in range(4) for j in range(2)
    ]


def query_side(slope, u_refs, k, row):
    acc = None
    for i, s in enumerate(slope):
        term = s[row : row + 1] * u_refs[i // 2][i % 2, k].astype(F32)
        acc = term if acc is None else acc + term
    return acc


def far_body(*refs):
    ms, st, u, q_refs = refs[:4], refs[4:8], refs[8:12], refs[12:14]
    coef_ref, dq_ref, lse_ref, loss_ref = refs[14:]
    lse, hot = line_rows(ms)
    slope = slopes(lse, st, q_refs)
    for i, s in enumerate(slope):
        coef_ref[i] = s * st[i // 2][i % 2, 1]
    for k in range(4):
        dq_ref[k] = query_side(slope, u, 4 + k, 4 + k).astype(BF16)
    lse_ref[0] = lse[:1]
    at = lax.broadcasted_iota(jnp.int32, (QR, QN), 0) == QT * lax.broadcasted_iota(jnp.int32, (QR, QN), 1)
    loss_ref[...] = jnp.dot(
        (lse - hot)[:1], at.astype(F32), preferred_element_type=F32, precision=lax.Precision.HIGHEST
    )


def far(ms, st, u, qs, after=()):
    return call(
        far_body,
        [((8, CH, QR), F32), ((4, W, QR), BF16), ((1, 1, QR), F32), ((1, QN), F32)],
        (*ms, *st, *u, *qs), name="far", flops=2**23, moved=2**21, after=after,
    )


def near_body(*refs):
    ms, st, u, q_refs, got_ref, outs = refs[:4], refs[4:8], refs[8:12], refs[12:14], refs[14], refs[15:]
    lse, _ = line_rows(ms)
    slope = slopes(lse, st, q_refs)
    for k in range(4):
        outs[k][...] = (query_side(slope, u, k, k) + got_ref[k].astype(F32)).astype(outs[k].dtype)


def near(ms, st, u, qs, got, after=()):
    return call(
        near_body, [((W, QR), F32)] + [((W, QR), BF16)] * 3,
        (*ms, *st, *u, *qs, got), name="near", flops=2**23, moved=2**21, after=after,
    )


def turn_body(*refs, skip):
    at = [(r, i) for r in refs[:-1] for i in range(r.shape[0])][skip:]
    for k, (ref, i) in enumerate(at):
        refs[-1][k] = ref[i, :QR, :].astype(F32).T.astype(BF16)


def turn(qs, name, skip=0):
    return call(
        functools.partial(turn_body, skip=skip), [((CH - skip, W, QR), BF16)], qs, name=name, flops=2**23, moved=2**20
    )[0]


def passage_side(e, coef, turned_ref):
    scaled = jnp.concatenate(
        [(turned_ref[k].astype(F32) * coef[k : k + 1]).astype(BF16) for k in range(turned_ref.shape[0])], axis=1
    )
    return lax.dot_general(e, scaled, NT, preferred_element_type=F32)


def back_body(e_ref, coef_ref, turned_ref, dp_ref, *, d):
    for j in range(2):
        dp_ref[j] = passage_side(e_ref[j], coef_ref[2 * d + j], turned_ref).astype(dp_ref.dtype)


def back(e, coef, turned, d, dtype, after=()):
    return call(
        functools.partial(back_body, d=d), [((2, SLOTS, W), dtype)], (e, coef, turned), name=f"back{d}",
        flops=2 * 2 * SLOTS * CH * QR * W, moved=5 * 2**20, after=after,
    )[0]


def back_neg_body(e_ref, sent_ref, got_ref, st_ref, za_ref, zb_ref, turned_ref, own_ref, dp_ref):
    rows = get_rows(sent_ref, 12) + get_rows(got_ref, 12)
    lse = jnp.concatenate([rows[3 * d] + rows[3 * d + 1] + rows[3 * d + 2] for d in ZORDER[1:]], axis=0)
    for j in range(2):
        hit = chosen((za_ref, zb_ref), j)
        coef = jnp.where(hit, jnp.exp(jnp.where(hit, st_ref[j, 0], LOW) - lse), 0.0) * st_ref[j, 1]
        dp_ref[j] = own_ref[j] + passage_side(e_ref[j], coef, turned_ref)


def back_neg(e, sent, got, st, zs, turned, own):
    return call(
        back_neg_body, [((2, SLOTS, W), F32)], (e, sent, got, st, *zs, turned, own), name="back_neg",
        flops=2 * 2 * SLOTS * CH * QR * W, moved=6 * 2**20,
    )[0]


def end_body(own_ref, g1, g2, g3, lse_ref, top_ref, n1, n2, dp_ref, p1, p2, p3, dq_out, dp_out):
    acc = own_ref[...]
    for g in (g1, g2, g3):
        acc = acc + g[...].astype(F32)
    acc = acc + jnp.exp(top_ref[...] - lse_ref[0]) * (n1[...].astype(F32) + n2[:W, :].astype(F32))
    dq_out[...] = acc.T.astype(BF16)
    acc = dp_ref[...]
    for g in (p1, p2, p3):
        acc = acc + g[...].astype(F32)
    dp_out[...] = acc.astype(BF16)


def end(own, got, lse, top, sums, dp, dp_got):
    return call(
        end_body, [((QR, W), BF16), ((2, SLOTS, W), BF16)], (own, *got, lse, top, *sums, dp, *dp_got), name="end",
        flops=2**20, moved=2**21,
    )


def shards(queries, passages, lengths, pos_ids, neg_ids):
    qx, px = pack(queries.reshape(QR, W), passages.reshape(2 * SLOTS, W), lengths, pos_ids, neg_ids)
    z2 = stack([qx, along_z(qx, 4)], "stack_z2")
    qa = stack([qx] + [along(qx, dx=d) for d in (1, 2, 3)], "stack_x", after=[z2])
    qs = (qa, along(qa, swap=1))
    pxs = [px] + [along(px, dy=d) for d in (1, 2, 3)]
    parts = [forward(qs, pxs[0], "forward0")]
    z4 = stack([z2, along_z(z2, 2)], "stack_z4", after=[parts[0][2]])
    zs = (z4, along_z(z4, 1))
    parts.append(forward(qs, pxs[1], "forward1", after=[z4]))
    e_n, u_n, st_n = forward(zs, px, "forward_neg", skip=1, after=[parts[1][2]])
    neg = neg_stats(st_n, zs)
    parts.append(forward(qs, pxs[2], "forward2", after=[neg]))
    neg = pair_up(neg, 4, parts[2][2])
    parts.append(forward(qs, pxs[3], "forward3", after=[neg]))
    neg = pair_up(neg, 2, parts[3][2])
    negs = (neg, along_z(neg, 1))
    es, us, sts = [p[0] for p in parts], [p[1] for p in parts], [p[2] for p in parts]
    turned, turned_n = turn(qs, "turn"), turn(zs, "turn_neg", 1)

    ms = local(sts, qs, *negs)
    top, send, keep = neg_sums(st_n, u_n, zs, *negs, after=[ms])
    ms = cores(ms, along(ms, swap=1))
    ms = [ms] + [along(ms, dx=d) for d in (1, 2, 3)]
    back_got = along_z(send, 1)
    coef, dq_far, lse, loss = far(ms, sts, us, qs, after=[back_got])

    lse_got = along_z(lse, 1)
    got = along(dq_far, swap=1)
    b2 = back(es[2], coef, turned, 2, BF16)
    sent, keep = halve(keep, back_got, lse, lse_got, "halve4", after=[b2])
    back_got = along_z(sent, 2)
    dqs = near(ms, sts, us, qs, got, after=[keep])
    dq_got = [along(dqs[r], dx=X - r) for r in (1, 2, 3)]
    b1 = back(es[1], coef, turned, 1, BF16, after=[dqs[0]])
    sent, keep = halve(keep, back_got, sent, back_got, "halve2", after=[b1, *dq_got])
    back_got = along_z(sent, 4)
    b3 = back(es[3], coef, turned, 3, BF16, after=[keep])
    dp_got = [along(b2, dy=2), along(b1, dy=3), along(b3, dy=1)]
    own = back(es[0], coef, turned, 0, F32, after=[b3, dp_got[0]])
    own = back_neg(e_n, sent, back_got, st_n, zs, turned_n, own)
    dq, dp = end(dqs[0], dq_got, lse, top, (keep, back_got), own, dp_got)
    return loss.reshape(QN), dq.reshape(QN, QT, W), dp


def solution(mesh):
    rows = P(("dp", "fsdp"))
    return jax.shard_map(
        shards, mesh=mesh, in_specs=(rows,) * 5, out_specs=(rows,) * 3, check_vma=False
    )
```

```python
import functools
import math

import jax
import jax.numpy as jnp
from jax import lax
from jax.experimental import pallas as pl
from jax.experimental.pallas import tpu as pltpu
from jax.sharding import PartitionSpec as P

F32, BF16 = jnp.float32, jnp.bfloat16
X, Y, C, Z = 4, 4, 2, 8
QN, QT, W, SLOTS, META = 8, 32, 128, 512, 16
QR = QN * QT
CH = 8
TEMP = 0.1
SCALE = 1.0 / TEMP * math.log2(math.e)
LOW = -1e30
ZORDER = (0, 4, 2, 6, 1, 5, 3, 7)
LIMIT = 8 * 1024 * 1024
NT = (((1,), (1,)), ((), ()))


def index(x, y, c):
    return ((x % X) * Y + (y % Y)) * C + c


def along(value, dx=0, dy=0, swap=0):
    pairs = [
        (index(x, y, c), index(x ^ dx, y ^ dy, c ^ swap))
        for x in range(X) for y in range(Y) for c in range(C)
    ]
    return lax.ppermute(value, "fsdp", pairs)


def along_z(value, flip):
    return lax.ppermute(value, "dp", [(z, z ^ flip) for z in range(Z)])


VMEM = pl.BlockSpec(memory_space=pltpu.VMEM)
ANY = pl.BlockSpec(memory_space=pl.ANY)


def call(body, outs, args, in_specs=None, scratch=(), name=None, flops=0, moved=0, exps=0, after=(), limit=LIMIT):
    n, m = len(args), len(after)

    def kernel(*refs):
        body(*refs[:n], *refs[n + m :])

    return pl.pallas_call(
        kernel,
        out_shape=[jax.ShapeDtypeStruct(s, d) for s, d in outs],
        in_specs=([VMEM] * n if in_specs is None else in_specs) + [ANY] * m,
        out_specs=[VMEM] * len(outs),
        scratch_shapes=list(scratch),
        compiler_params=pltpu.CompilerParams(vmem_limit_bytes=limit),
        cost_estimate=pl.CostEstimate(flops=flops, bytes_accessed=moved, transcendentals=exps),
        name=name,
    )(*args, *after)


def pack_body(
    q_ref, p_ref, len_hbm, pos_hbm, neg_hbm, qx_ref, px_ref, len_ref, pos_ref, neg_ref, sems
):
    copies = [
        pltpu.make_async_copy(len_hbm, len_ref, sems.at[0]),
        pltpu.make_async_copy(pos_hbm, pos_ref, sems.at[1]),
        pltpu.make_async_copy(neg_hbm, neg_ref, sems.at[2]),
        pltpu.make_async_copy(q_ref, qx_ref.at[pl.ds(0, QR)], sems.at[3]),
        pltpu.make_async_copy(p_ref, px_ref.at[pl.ds(0, 2 * SLOTS)], sems.at[4]),
    ]
    for c in copies:
        c.start()
    for c in copies[:4]:
        c.wait()
    lane = lax.broadcasted_iota(jnp.int32, (META, W), 1) // QT
    row = lax.broadcasted_iota(jnp.int32, (META, W), 0)
    acc = jnp.zeros((META, W), jnp.int32)
    per = W // QT
    for q in range(QN):
        here = lane == q % per
        acc = jnp.where(here & (row == q // per), pos_ref[q], acc)
        for a in range(4):
            code = (neg_ref[a, q] // (2 * X * Y * C)) * 2 + neg_ref[a, q] % 2
            acc = jnp.where(here & (row == 2 + 2 * a + q // per), code, acc)
    qx_ref[QR:, :] = acc.astype(F32).astype(BF16)
    acc = jnp.zeros((META, W), jnp.int32)
    for j in range(2):
        acc = jnp.where(row == 2 * j, len_ref[j] // 16, acc)
        acc = jnp.where(row == 2 * j + 1, len_ref[j] % 16, acc)
    px_ref[2 * SLOTS :, :] = acc.astype(F32).astype(BF16)
    copies[4].wait()


def pack(q, p, lengths, pos, neg):
    return call(
        pack_body,
        [((QR + META, W), BF16), ((2 * SLOTS + META, W), BF16)],
        (q, p, lengths, pos, neg.T), [ANY] * 5,
        [
            pltpu.SMEM((2,), jnp.int32), pltpu.SMEM((QN,), jnp.int32), pltpu.SMEM((4, QN), jnp.int32),
            pltpu.SemaphoreType.DMA((5,)),
        ],
        name="pack", moved=2**20, limit=63_143_936,
    )


def stack_body(*refs):
    at = 0
    for ref in refs[:-1]:
        n = ref.shape[0] if ref.ndim == 3 else 1
        refs[-1][at : at + n] = ref[...].reshape(n, *ref.shape[-2:])
        at += n


def stack(parts, name, after=()):
    n = sum(p.shape[0] if p.ndim == 3 else 1 for p in parts)
    return call(stack_body, [((n, *parts[0].shape[-2:]), parts[0].dtype)], parts, name=name, moved=2**19, after=after)[0]


def forward_body(*refs, skip):
    q_refs, (p_ref, e_ref, u_ref, st_ref) = refs[:-4], refs[-4:]
    q_at = [(r, i) for r in q_refs for i in range(r.shape[0])][skip:]
    chunks = len(q_at)
    meta = p_ref[2 * SLOTS :, :].astype(F32)
    slot = lax.broadcasted_iota(jnp.int32, (SLOTS, W), 0).astype(F32)
    pick = (lax.broadcasted_iota(jnp.int32, (QR, W), 1) == 0).astype(F32).astype(BF16)
    wide, turned = [], []
    for j in range(2):
        p = p_ref[j * SLOTS : (j + 1) * SLOTS, :]
        length = meta[2 * j : 2 * j + 1] * 16 + meta[2 * j + 1 : 2 * j + 2]
        bias = jnp.where(slot < length, 0.0, LOW).astype(BF16)
        wide.append(jnp.concatenate([p, bias], axis=1))
        turned.append(jnp.concatenate([p.astype(F32).T, jnp.ones((16, SLOTS), F32)], axis=0).astype(BF16))
    rows = [[None] * chunks for _ in range(2)]

    def product(j, k):
        ref, i = q_at[k]
        qk = jnp.concatenate([ref[i, :QR, :], pick], axis=1)
        return lax.dot_general(wide[j], qk, NT, preferred_element_type=F32)

    def finish(j, k, top, e):
        u = jnp.dot(turned[j], e, preferred_element_type=F32)
        total = u[W : W + 1]
        inverse = 1.0 / total
        u_ref[j, k] = (u[:W] * inverse).astype(BF16)
        st_ref[j, 1, k : k + 1, :] = inverse
        rows[j][k] = top + TEMP * jnp.log(total)

    tiles = [(j, k) for j in range(2) for k in range(chunks)]
    s, waiting = product(*tiles[0]), []
    for i, (j, k) in enumerate(tiles):
        later = product(*tiles[i + 1]) if i + 1 < len(tiles) else None
        top = jnp.max(s, axis=0, keepdims=True)
        e = jnp.exp2((s - top) * SCALE).astype(BF16)
        e_ref[j, :, k * QR : (k + 1) * QR] = e
        waiting.append((j, k, top, e))
        if len(waiting) > 2:
            finish(*waiting.pop(0))
        s = later
    for w in waiting:
        finish(*w)
    same = (
        lax.broadcasted_iota(jnp.int32, (W, W), 0) // QT == lax.broadcasted_iota(jnp.int32, (W, W), 1) // QT
    ).astype(F32)
    both = jnp.concatenate([r[:, h * W : (h + 1) * W] for j in range(2) for h in range(2) for r in rows[j]], axis=0)
    score = jnp.dot(both, same, preferred_element_type=F32, precision=lax.Precision.HIGHEST)
    for j in range(2):
        for h in range(2):
            st_ref[j, 0, :, h * W : (h + 1) * W] = score[(2 * j + h) * chunks : (2 * j + h + 1) * chunks]


def forward(qs, px, name, skip=0, after=()):
    chunks = CH - skip
    work = 2 * SLOTS * chunks * QR
    return call(
        functools.partial(forward_body, skip=skip),
        [((2, SLOTS, chunks * QR), BF16), ((2, chunks, W, QR), BF16), ((2, 2, chunks, QR), F32)],
        (*qs, px), name=name, flops=8 * work * W, moved=7 * 2**20, exps=work, after=after,
    )


def meta_rows(q_refs, first):
    rows = []
    for ref in q_refs:
        for i in range(ref.shape[0]):
            m = ref[i, QR:, :].astype(F32)
            rows.append(jnp.concatenate([m[first : first + 1], m[first + 1 : first + 2]], axis=1))
    return jnp.concatenate(rows, axis=0)


def group_index(dy, j):
    f = lax.axis_index("fsdp")
    x, y, c = f // (Y * C), f // C % Y, f % C
    return (((x * Y + (y ^ dy)) * C + c) * 2 + j).astype(F32)


def chosen(z_refs, j):
    code = (lax.axis_index("dp") * 2 + j).astype(F32)
    hit = meta_rows(z_refs, 2)[1:] == code
    for a in range(1, 4):
        hit = hit | (meta_rows(z_refs, 2 + 2 * a)[1:] == code)
    return hit


def chosen_scores(st_ref, z_refs):
    hits = [chosen(z_refs, j) for j in range(2)]
    return hits, [jnp.where(hits[j], st_ref[j, 0], LOW) for j in range(2)]


def neg_stats_body(st_ref, za_ref, zb_ref, out_ref):
    hits, scores = chosen_scores(st_ref, (za_ref, zb_ref))
    top = jnp.maximum(scores[0], scores[1])
    total = sum(jnp.where(h, jnp.exp(s - top), 0.0) for h, s in zip(hits, scores))
    out_ref[:, :QR] = jnp.concatenate([jnp.full((1, QR), LOW, F32), top], axis=0)
    out_ref[:, QR:] = jnp.concatenate([jnp.zeros((1, QR), F32), total], axis=0)


def neg_stats(st, zs):
    return call(neg_stats_body, [((Z, 2 * QR), F32)], (st, *zs), name="neg_stats", flops=2**16, moved=2**17)[0]


def pair(a, b, flip):
    rows = [ZORDER.index(d ^ flip) for d in ZORDER]
    b = jnp.concatenate([b[r : r + 1] for r in rows], axis=0)
    top = jnp.maximum(a[:, :QR], b[:, :QR])
    return top, a[:, QR:] * jnp.exp(a[:, :QR] - top) + b[:, QR:] * jnp.exp(b[:, :QR] - top)


def pair_body(a_ref, b_ref, out_ref, *, flip):
    out_ref[:, :QR], out_ref[:, QR:] = pair(a_ref[...], b_ref[...], flip)


def pair_up(a, flip, after):
    return call(
        functools.partial(pair_body, flip=flip), [((Z, 2 * QR), F32)], (a, along_z(a, flip)), name=f"pair{flip}",
        flops=2**16, moved=2**16, after=[after],
    )[0]


def split3(v):
    high = v.astype(BF16)
    rest = v - high.astype(F32)
    middle = rest.astype(BF16)
    return [high.astype(F32), middle.astype(F32), rest - middle.astype(F32)]


def put_rows(ref, rows):
    rows = jnp.concatenate([*rows, jnp.zeros((META - len(rows), QR), F32)], axis=0)
    ref[ref.shape[0] - META :, :] = rows.astype(BF16)


def get_rows(ref, n):
    tail = ref[ref.shape[0] - META :, :].astype(F32)
    return [tail[i : i + 1] for i in range(n)]


def neg_sums_body(st_ref, u_ref, za_ref, zb_ref, a_ref, b_ref, top_ref, send_ref, keep_ref):
    top, _ = pair(a_ref[...], b_ref[...], 1)
    top_ref[...] = top[:1]
    hits, scores = chosen_scores(st_ref, (za_ref, zb_ref))
    w = [jnp.where(h, jnp.exp(s - top[1:]), 0.0) for h, s in zip(hits, scores)]
    for n, d in enumerate((0, 2, 4, 6)):
        for ref, i in ((keep_ref, ZORDER.index(d)), (send_ref, ZORDER.index(d + 1))):
            if d or ref is send_ref:
                sums = [w[j][i - 1 : i] * u_ref[j, i - 1].astype(F32) for j in range(2)]
                ref[n * W : (n + 1) * W, :] = (sums[0] + sums[1]).astype(BF16)
            else:
                ref[n * W : (n + 1) * W, :] = jnp.zeros((W, QR), BF16)


def neg_sums(st, u, zs, a, b, after=()):
    return call(
        neg_sums_body, [((1, QR), F32)] + [((4 * W, QR), BF16)] * 2, (st, u, *zs, a, b),
        name="neg_sums", flops=2**20, moved=2**21, after=after,
    )


def halve_body(keep_ref, got_ref, a_ref, b_ref, send_out, keep_out):
    n = keep_out.shape[0] // W
    for i in range(n):
        for ref, k in ((keep_out, 2 * i), (send_out, 2 * i + 1)):
            at = slice(k * W, (k + 1) * W)
            ref[i * W : (i + 1) * W, :] = (keep_ref[at, :].astype(F32) + got_ref[at, :].astype(F32)).astype(BF16)
    if n == 2:
        rows = split3(a_ref[0]) + split3(b_ref[0])
    else:
        rows = get_rows(a_ref, 6) + get_rows(b_ref, 6)
    put_rows(send_out, rows)


def halve(keep, got, a, b, name, after=()):
    n = keep.shape[0] // 2
    return call(
        halve_body, [((n + META, QR), BF16), ((n, QR), BF16)], (keep, got, a, b), name=name, flops=2**18, moved=2**20,
        after=after,
    )


def local_body(*refs):
    st_refs, q_refs, a_ref, b_ref, out_ref = refs[:4], refs[4:6], refs[6], refs[7], refs[8]
    scores = [st_refs[d][j, 0] for d in range(4) for j in range(2)]
    gids = [group_index(d, j) for d in range(4) for j in range(2)]
    pos = meta_rows(q_refs, 0)
    top = functools.reduce(jnp.maximum, scores)
    total = sum(jnp.exp(s - top) for s in scores)
    hot = sum(jnp.where(pos == g, s, 0.0) for s, g in zip(scores, gids))
    top_n, total_n = (v[:1] for v in pair(a_ref[...], b_ref[...], 1))
    new = jnp.maximum(top[:1], top_n)
    first = total[:1] * jnp.exp(top[:1] - new) + total_n * jnp.exp(top_n - new)
    out_ref[:, :QR] = jnp.concatenate([new, top[1:]], axis=0)
    out_ref[:, QR : 2 * QR] = jnp.concatenate([first, total[1:]], axis=0)
    out_ref[:, 2 * QR :] = hot


def local(stats, qs, a, b):
    return call(local_body, [((CH, 3 * QR), F32)], (*stats, *qs, a, b), name="local", flops=2**20, moved=2**18)[0]


def merge(parts):
    top = functools.reduce(jnp.maximum, [p[:, :QR] for p in parts])
    total = sum(p[:, QR : 2 * QR] * jnp.exp(p[:, :QR] - top) for p in parts)
    return top, total, sum(p[:, 2 * QR :] for p in parts)


def cores_body(a_ref, b_ref, out_ref):
    a, b = a_ref[...], b_ref[...]
    parts = merge([a, jnp.concatenate([b[4:], b[:4]], axis=0)])
    for i, v in enumerate(parts):
        out_ref[:, i * QR : (i + 1) * QR] = v


def cores(a, b, after=()):
    return call(cores_body, [((CH, 3 * QR), F32)], (a, b), name="cores", flops=2**16, moved=2**17)[0]


def line_rows(refs):
    parts = []
    for dx, ref in enumerate(refs):
        v = ref[...]
        order = [(r ^ dx) + h for h in (0, 4) for r in range(4)]
        parts.append(jnp.concatenate([v[o : o + 1] for o in order], axis=0) if dx else v)
    top, total, hot = merge(parts)
    return top + jnp.log(total), hot


def slopes(lse, st_refs, q_refs):
    pos = meta_rows(q_refs, 0)
    return [
        jnp.exp(st_refs[d][j, 0] - lse) - (pos == group_index(d, j)).astype(F32)
        for d in range(4) for j in range(2)
    ]


def query_side(slope, u_refs, k, row):
    acc = None
    for i, s in enumerate(slope):
        term = s[row : row + 1] * u_refs[i // 2][i % 2, k].astype(F32)
        acc = term if acc is None else acc + term
    return acc


def far_body(*refs):
    ms, st, u, q_refs = refs[:4], refs[4:8], refs[8:12], refs[12:14]
    coef_ref, dq_ref, lse_ref, loss_ref = refs[14:]
    lse, hot = line_rows(ms)
    slope = slopes(lse, st, q_refs)
    for i, s in enumerate(slope):
        coef_ref[i] = s * st[i // 2][i % 2, 1]
    for k in range(4):
        dq_ref[k] = query_side(slope, u, 4 + k, 4 + k).astype(BF16)
    lse_ref[0] = lse[:1]
    at = lax.broadcasted_iota(jnp.int32, (QR, QN), 0) == QT * lax.broadcasted_iota(jnp.int32, (QR, QN), 1)
    loss_ref[...] = jnp.dot(
        (lse - hot)[:1], at.astype(F32), preferred_element_type=F32, precision=lax.Precision.HIGHEST
    )


def far(ms, st, u, qs, after=()):
    return call(
        far_body,
        [((8, CH, QR), F32), ((4, W, QR), BF16), ((1, 1, QR), F32), ((1, QN), F32)],
        (*ms, *st, *u, *qs), name="far", flops=2**23, moved=2**21, after=after,
    )


def near_body(*refs):
    ms, st, u, q_refs, got_ref, keep_ref, send_ref = refs[:4], refs[4:8], refs[8:12], refs[12:14], *refs[14:]
    lse, _ = line_rows(ms)
    slope = slopes(lse, st, q_refs)
    for k in range(4):
        v = query_side(slope, u, k, k) + got_ref[k].astype(F32)
        if k < 2:
            keep_ref[k] = v
        else:
            send_ref[k - 2] = v.astype(BF16)


def near(ms, st, u, qs, got, after=()):
    return call(
        near_body, [((2, W, QR), F32), ((2, W, QR), BF16)],
        (*ms, *st, *u, *qs, got), name="near", flops=2**23, moved=2**21, after=after,
    )


def join_body(keep_ref, got_ref, keep_out, send_out):
    keep_out[...] = keep_ref[0] + got_ref[0].astype(F32)
    send_out[...] = (keep_ref[1] + got_ref[1].astype(F32)).astype(BF16)


def join(keep, got, after=()):
    return call(
        join_body, [((W, QR), F32), ((W, QR), BF16)], (keep, got), name="join", flops=2**17, moved=2**18, after=after
    )


def turn_body(*refs, skip):
    at = [(r, i) for r in refs[:-1] for i in range(r.shape[0])][skip:]
    for k, (ref, i) in enumerate(at):
        refs[-1][k] = ref[i, :QR, :].astype(F32).T.astype(BF16)


def turn(qs, name, skip=0):
    return call(
        functools.partial(turn_body, skip=skip), [((CH - skip, W, QR), BF16)], qs, name=name, flops=2**23, moved=2**20
    )[0]


def passage_side(e, coef, turned_ref):
    scaled = jnp.concatenate(
        [(turned_ref[k].astype(F32) * coef[k : k + 1]).astype(BF16) for k in range(turned_ref.shape[0])], axis=1
    )
    return lax.dot_general(e, scaled, NT, preferred_element_type=F32)


def back_body(e_ref, coef_ref, turned_ref, dp_ref, *, d):
    for j in range(2):
        dp_ref[j] = passage_side(e_ref[j], coef_ref[2 * d + j], turned_ref).astype(dp_ref.dtype)


def back(e, coef, turned, d, dtype, after=()):
    return call(
        functools.partial(back_body, d=d), [((2, SLOTS, W), dtype)], (e, coef, turned), name=f"back{d}",
        flops=2 * 2 * SLOTS * CH * QR * W, moved=5 * 2**20, after=after,
    )[0]


def back_neg_body(e_ref, sent_ref, got_ref, st_ref, za_ref, zb_ref, turned_ref, own_ref, dp_ref):
    rows = get_rows(sent_ref, 12) + get_rows(got_ref, 12)
    lse = jnp.concatenate([rows[3 * d] + rows[3 * d + 1] + rows[3 * d + 2] for d in ZORDER[1:]], axis=0)
    for j in range(2):
        hit = chosen((za_ref, zb_ref), j)
        coef = jnp.where(hit, jnp.exp(jnp.where(hit, st_ref[j, 0], LOW) - lse), 0.0) * st_ref[j, 1]
        dp_ref[j] = own_ref[j] + passage_side(e_ref[j], coef, turned_ref)


def back_neg(e, sent, got, st, zs, turned, own):
    return call(
        back_neg_body, [((2, SLOTS, W), F32)], (e, sent, got, st, *zs, turned, own), name="back_neg",
        flops=2 * 2 * SLOTS * CH * QR * W, moved=6 * 2**20,
    )[0]


def end_body(own_ref, got_ref, lse_ref, top_ref, n1, n2, dp_ref, p1, p2, p3, dq_out, dp_out):
    acc = own_ref[...] + got_ref[...].astype(F32)
    acc = acc + jnp.exp(top_ref[...] - lse_ref[0]) * (n1[...].astype(F32) + n2[:W, :].astype(F32))
    dq_out[...] = acc.T.astype(BF16)
    acc = dp_ref[...]
    for g in (p1, p2, p3):
        acc = acc + g[...].astype(F32)
    dp_out[...] = acc.astype(BF16)


def end(own, got, lse, top, sums, dp, dp_got):
    return call(
        end_body, [((QR, W), BF16), ((2, SLOTS, W), BF16)], (own, got, lse, top, *sums, dp, *dp_got), name="end",
        flops=2**20, moved=2**21,
    )


def shards(queries, passages, lengths, pos_ids, neg_ids):
    qx, px = pack(queries.reshape(QR, W), passages.reshape(2 * SLOTS, W), lengths, pos_ids, neg_ids)
    z2 = stack([qx, along_z(qx, 4)], "stack_z2")
    qa = stack([qx] + [along(qx, dx=d) for d in (1, 2, 3)], "stack_x", after=[z2])
    qs = (qa, along(qa, swap=1))
    pxs = [px] + [along(px, dy=d) for d in (1, 2, 3)]
    parts = [forward(qs, pxs[0], "forward0")]
    z4 = stack([z2, along_z(z2, 2)], "stack_z4", after=[parts[0][2]])
    zs = (z4, along_z(z4, 1))
    parts.append(forward(qs, pxs[1], "forward1", after=[z4]))
    e_n, u_n, st_n = forward(zs, px, "forward_neg", skip=1, after=[parts[1][2]])
    neg = neg_stats(st_n, zs)
    parts.append(forward(qs, pxs[2], "forward2", after=[neg]))
    neg = pair_up(neg, 4, parts[2][2])
    parts.append(forward(qs, pxs[3], "forward3", after=[neg]))
    neg = pair_up(neg, 2, parts[3][2])
    negs = (neg, along_z(neg, 1))
    es, us, sts = [p[0] for p in parts], [p[1] for p in parts], [p[2] for p in parts]
    turned, turned_n = turn(qs, "turn"), turn(zs, "turn_neg", 1)

    ms = local(sts, qs, *negs)
    top, send, keep = neg_sums(st_n, u_n, zs, *negs, after=[ms])
    ms = cores(ms, along(ms, swap=1))
    ms = [ms] + [along(ms, dx=d) for d in (1, 2, 3)]
    back_got = along_z(send, 1)
    coef, dq_far, lse, loss = far(ms, sts, us, qs, after=[back_got])

    lse_got = along_z(lse, 1)
    got = along(dq_far, swap=1)
    b2 = back(es[2], coef, turned, 2, BF16)
    sent, keep = halve(keep, back_got, lse, lse_got, "halve4", after=[b2])
    back_got = along_z(sent, 2)
    dq_keep, dq_send = near(ms, sts, us, qs, got, after=[keep])
    b1 = back(es[1], coef, turned, 1, BF16, after=[dq_keep])
    dq_own, dq_send = join(dq_keep, along(dq_send, dx=2), after=[b1])
    dq_got = along(dq_send, dx=1)
    sent, keep = halve(keep, back_got, sent, back_got, "halve2", after=[dq_own])
    back_got = along_z(sent, 4)
    b3 = back(es[3], coef, turned, 3, BF16, after=[keep])
    dp_got = [along(b2, dy=2), along(b1, dy=1), along(b3, dy=3)]
    own = back(es[0], coef, turned, 0, F32, after=[b3, dp_got[0]])
    own = back_neg(e_n, sent, back_got, st_n, zs, turned_n, own)
    dq, dp = end(dq_own, dq_got, lse, top, (keep, back_got), own, dp_got)
    return loss.reshape(QN), dq.reshape(QN, QT, W), dp


def solution(mesh):
    rows = P(("dp", "fsdp"))
    return jax.shard_map(
        shards, mesh=mesh, in_specs=(rows,) * 5, out_specs=(rows,) * 3, check_vma=False
    )
```
